512 devices in a mesh: dp: 8 (over x, z_lo), section: 4 (over z_hi), tensor: 16 (over y, core).
Axes of the slice: x: 4, y: 8, z: 8 (z_hi: 4, z_lo: 2; z = z_hi * 2 + z_lo), core: 2. Of those that a mesh axis runs over, the one named last changes fastest.
Arguments:
- passed_activations: bfloat16 [4, 2048, 3072], P('section', 'dp', 'tensor'), may hold values from -6 to 6
- kept_section_input: bfloat16 [4, 2048, 3072], P('section', 'dp', 'tensor'), may hold values from -47 to 47
- handed_grads: bfloat16 [4, 2048, 3072], P('section', 'dp', 'tensor'), may hold values from -6 to 6
- norm_gain: float32 [4, 3072], P('section'), may hold values from 0.1 to 6
- gate_weight: bfloat16 [4, 3072, 5376], P('section', 'dp', 'tensor'), may hold values from -0.109375 to 0.109375
- up_weight: bfloat16 [4, 3072, 5376], P('section', 'dp', 'tensor'), may hold values from -0.109375 to 0.109375
- down_weight: bfloat16 [4, 5376, 3072], P('section', 'tensor', 'dp'), may hold values from -0.078125 to 0.078125
- routes: int32 [4, 2, 2048, 4], P('section', None, 'dp'), may hold values from 0 to 15, all different within a row
- route_probs: float32 [4, 2, 2048, 4], P('section', None, 'dp'), may hold values from 0.1 to 1
Outputs:
- section_output: bfloat16 [4, 2048, 3072], P('section', 'dp', 'tensor')
- stored_input_gradient: bfloat16 [4, 2048, 3072], P('section', 'dp', 'tensor')
- gate_grad: bfloat16 [4, 3072, 5376], P('section', None, 'tensor')
- up_grad: bfloat16 [4, 3072, 5376], P('section', None, 'tensor')
The draws below stay inside these ranges and needn't reach their ends.
Inputs may be any that keep to these rules, and one draw needn't show every extreme that they name: `routes`: each row names 4 different experts, and every expert is named somewhere.
All inputs are finite; a program needn't handle non-finite values.
Results may differ from the reference program's by a relative error of at most 0.018.
Values may be sent and summed in bfloat16 or wider, within the bound.
No kernel may reach another device: no remote copies, remote signals or barrier semaphores. Data moves between devices by JAX's collectives and lax.ppermute only.
A program may use at most 128 MiB of HBM per device.

```python
import jax
import jax.numpy as jnp
from jax import lax

D = 3072
FF = 5376
EXPERTS = 16
TOP = 4
TOK_DEV = 256
TOKENS = 2048
SECTIONS = 4
N_DP = 8
N_SECTION = 4
N_TENSOR = 16


def rising_profile(key, low_log, high_log, rough_low, rough_high):
    ramp = jnp.linspace(low_log, high_log, D, dtype=jnp.float32)
    rough = jax.random.uniform(key, (SECTIONS, D), jnp.float32, rough_low, rough_high)
    return jnp.exp(ramp)[None, :] * rough


def draw_norm_gain(key, part):
    key = jax.random.fold_in(key, 11)
    return rising_profile(key, jnp.log(0.3), jnp.log(3.0), 0.7, 1.3)


def draw_kept_section_input(key, part):
    key = jax.random.fold_in(key, 23)
    first = jax.random.fold_in(key, 0)
    values = jnp.clip(jax.random.normal(first, (SECTIONS, TOKENS, D), jnp.float32), -6.0, 6.0)
    column_scale = jnp.exp(jnp.linspace(0.0, jnp.log(4.0), D, dtype=jnp.float32))[None, :] * jnp.ones((SECTIONS, 1), jnp.float32)
    return (values * column_scale[:, None, :]).astype(jnp.bfloat16)


def level_of(rng, extent, cuts, low, high):
    gain, own = 1.0, jax.random.fold_in(rng, 6)
    for dim, blocks in cuts:
        draws = jnp.exp(jax.random.uniform(jax.random.fold_in(own, dim), (blocks,), jnp.float32, low / len(cuts), high / len(cuts)))
        gain = gain * jnp.repeat(draws, extent[dim] // blocks).reshape([-1 if axis == dim else 1 for axis in range(len(extent))])
    return gain


def picks_of(own_key, rows, count, top, lift):
    ranking = jax.random.permutation(jax.random.fold_in(own_key, 1), count)
    boost = ranking
    for power in range(3):
        boost = boost * boost // count
    boost = boost * lift // count
    tickets = jax.random.randint(jax.random.fold_in(own_key, 2), (rows, count), 0, 4096) + boost
    holders = jax.random.permutation(jax.random.fold_in(own_key, 3), rows)[jnp.arange(count) % rows]
    tickets = jnp.where(jnp.arange(rows)[:, None] == holders[None, :], 1 << 14, tickets)
    priority = tickets * count + jnp.arange(count)
    return lax.top_k(priority.astype(jnp.int32), top)[1].astype(jnp.int32)


def bell_draw(stream_key, extent, spread, reach, shards=(), kind=jnp.bfloat16):
    gain = level_of(stream_key, extent, shards, -0.22, 0.18) if shards else 1.0
    result = jax.random.normal(stream_key, extent, jnp.float32) * spread * gain
    return jnp.minimum(jnp.maximum(result, -reach), reach).astype(kind)


def setup_inputs(seed: int = 0) -> dict:
    keys = jax.random.split(jax.random.key(seed), 10)
    return {
        "passed_activations": bell_draw(keys[0], (SECTIONS, TOKENS, D), 1.0, 6.0, ((0, 4), (1, 8), (2, 16))),
        "kept_section_input": draw_kept_section_input(jax.random.fold_in(keys[9], 71), 0),
        "handed_grads": bell_draw(keys[2], (SECTIONS, TOKENS, D), 1.0, 6.0, ((0, 4), (1, 8), (2, 16))),
        "norm_gain": draw_norm_gain(jax.random.fold_in(keys[9], 71), 0),
        "gate_weight": bell_draw(keys[4], (SECTIONS, D, FF), D ** -0.5, 0.109375, ((0, 4), (1, 8), (2, 16))),
        "up_weight": bell_draw(keys[5], (SECTIONS, D, FF), D ** -0.5, 0.109375, ((0, 4), (1, 8), (2, 16))),
        "down_weight": bell_draw(keys[6], (SECTIONS, FF, D), FF ** -0.5, 0.078125, ((0, 4), (1, 16), (2, 8))),
        "routes": picks_of(keys[7], SECTIONS * 2 * TOKENS, EXPERTS, TOP, 4096).reshape((SECTIONS, 2, TOKENS, TOP)),
        "route_probs": jnp.clip(0.1 + 0.9 * jax.random.uniform(keys[8], (SECTIONS, 2, TOKENS, TOP), jnp.float32) ** level_of(keys[8], (SECTIONS, 2, TOKENS, TOP), ((0, 4), (2, 8)), -0.2, 0.2), 0.1, 1.0),
    }


EPS = 1e-05

def rounded(value):
    return lax.optimization_barrier(value.astype(jnp.bfloat16)).astype(jnp.float32)

def normalized_input(inputs, norm_scale_weight):
    float_input = inputs.astype(jnp.float32)
    inverse_norm_scale = lax.rsqrt(lax.optimization_barrier(jnp.mean(float_input * float_input, axis=-1, keepdims=True)) + EPS)
    normalized_values = float_input * inverse_norm_scale
    return (float_input, inverse_norm_scale, normalized_values, (normalized_values * norm_scale_weight[None, :]).astype(jnp.bfloat16))

def combine(route_ids, probs):
    return lax.optimization_barrier(jnp.sum(jnp.where(route_ids == 0, probs, jnp.zeros_like(probs)), axis=-1))

def reference(passed_activations, kept_section_input, handed_grads, norm_gain, gate_weight, up_weight, down_weight, routes, route_probs):
    group = FF // N_TENSOR
    outputs = []
    incoming_gradients = []
    gate_grads = []
    up_grads = []
    for section_index in range(N_SECTION):
        w_gate = gate_weight[section_index]
        w_up = up_weight[section_index]
        w_down = down_weight[section_index]
        norm_scale_weight = norm_gain[section_index]
        weight_f = combine(routes[section_index, 0], route_probs[section_index, 0])
        float_input, inverse_norm_scale, normalized_values, normalized_rows = normalized_input(passed_activations[(section_index - 1) % N_SECTION], norm_scale_weight)
        gate_pre = jnp.dot(normalized_rows, w_gate, preferred_element_type=jnp.float32)
        up_pre = jnp.dot(normalized_rows, w_up, preferred_element_type=jnp.float32)
        hidden = (jax.nn.silu(gate_pre) * up_pre * weight_f[:, None]).astype(jnp.bfloat16)
        summed = jnp.zeros((TOKENS, D), jnp.float32)
        for part in range(N_TENSOR):
            low = part * group
            summed = summed + rounded(jnp.dot(hidden[:, low:low + group], w_down[low:low + group], preferred_element_type=jnp.float32))
        outputs.append((float_input + summed).astype(jnp.bfloat16))
        weight_b = combine(routes[section_index, 1], route_probs[section_index, 1])
        incoming_output_gradient = handed_grads[(section_index + 1) % N_SECTION]
        float_input_backward, inverse_norm_backward, normalized_values_backward, normalized_rows_backward = normalized_input(kept_section_input[section_index], norm_scale_weight)
        gate_b = jnp.dot(normalized_rows_backward, w_gate, preferred_element_type=jnp.float32)
        up_b = jnp.dot(normalized_rows_backward, w_up, preferred_element_type=jnp.float32)
        hidden_grad = jnp.dot(incoming_output_gradient, w_down.T, preferred_element_type=jnp.float32)
        sigmoid_g = jax.nn.sigmoid(gate_b)
        active = gate_b * sigmoid_g
        slope = sigmoid_g * (1.0 + gate_b * (1.0 - sigmoid_g))
        dgate = (hidden_grad * weight_b[:, None] * up_b * slope).astype(jnp.bfloat16)
        dup = (hidden_grad * weight_b[:, None] * active).astype(jnp.bfloat16)
        dnormal = jnp.zeros((TOKENS, D), jnp.float32)
        for part in range(N_TENSOR):
            low = part * group
            term = jnp.dot(dgate[:, low:low + group], w_gate[:, low:low + group].T, preferred_element_type=jnp.float32)
            term = term + jnp.dot(dup[:, low:low + group], w_up[:, low:low + group].T, preferred_element_type=jnp.float32)
            dnormal = dnormal + rounded(term)
        normalized_input_gradient = dnormal * norm_scale_weight[None, :]
        mean_square_stat = lax.optimization_barrier(jnp.mean(normalized_input_gradient * normalized_values_backward, axis=-1, keepdims=True))
        incoming_gradients.append((incoming_output_gradient.astype(jnp.float32) + inverse_norm_backward * (normalized_input_gradient - normalized_values_backward * mean_square_stat)).astype(jnp.bfloat16))
        grad_g = jnp.zeros((D, FF), jnp.float32)
        grad_u = jnp.zeros((D, FF), jnp.float32)
        for replica in range(N_DP):
            low = replica * TOK_DEV
            rows_n = normalized_rows_backward[low:low + TOK_DEV]
            grad_g = grad_g + rounded(jnp.dot(rows_n.T, dgate[low:low + TOK_DEV], preferred_element_type=jnp.float32))
            grad_u = grad_u + rounded(jnp.dot(rows_n.T, dup[low:low + TOK_DEV], preferred_element_type=jnp.float32))
        gate_grads.append(grad_g.astype(jnp.bfloat16))
        up_grads.append(grad_u.astype(jnp.bfloat16))
    return (jnp.stack(outputs), jnp.stack(incoming_gradients), jnp.stack(gate_grads), jnp.stack(up_grads))
```

```python
import jax
import jax.numpy as jnp
import numpy as np
from jax import lax
from jax.experimental import pallas as pl
from jax.experimental.pallas import tpu as pltpu
from jax.sharding import Mesh, PartitionSpec as P

EPS = 1e-05
AXES = ("x", "zl", "s", "y", "c")
SIZES = {"x": 4, "zl": 2, "s": 4, "y": 8, "c": 2}
D = 3072
TOK = 256
G = 336
F = 192
N_T = 16
N_DP = 8
DS = D // N_DP
OFFSETS = ((0, 0), (0, 1), (-1, 0), (1, 0), (-1, 1), (1, 1), (2, 0), (2, 1))
VMEM_LIMIT = 50 * 1024 * 1024

VM = pl.BlockSpec(memory_space=pltpu.VMEM)
SM = pl.BlockSpec(memory_space=pltpu.SMEM)
HB = pl.BlockSpec(memory_space=pl.ANY)


def shift(value, **steps):
    axes = tuple(a for a in AXES if a in steps)
    sizes = [SIZES[a] for a in axes]
    pairs = []
    for i in range(int(np.prod(sizes))):
        at = np.unravel_index(i, sizes)
        to = [(at[k] + steps[a]) % sizes[k] for k, a in enumerate(axes)]
        pairs.append((i, int(np.ravel_multi_index(to, sizes))))
    return lax.ppermute(value, axes if len(axes) > 1 else axes[0], pairs)


def swapped(value, step):
    pairs = []
    for e in range(N_DP):
        for y in range(N_DP):
            d = (((y // 2) + step) % 4) * 2 + y % 2
            pairs.append((e * N_DP + y, d * N_DP + e))
    return lax.ppermute(value, ("x", "zl", "y"), pairs)


def gather_ring(own):
    z = shift(own, zl=1)
    behind = shift(own, x=1)
    ahead = shift(own, x=-1)
    z, behind, ahead = lax.optimization_barrier((z, behind, ahead))
    z_behind = shift(z, x=1)
    z_ahead = shift(z, x=-1)
    across = shift(behind, x=1)
    z_across = shift(z_ahead, x=-1)
    return [own, z, behind, ahead, z_behind, z_ahead, across, z_across]


def places():
    x, zl = lax.axis_index("x"), lax.axis_index("zl")
    return jnp.stack([((x + dx) % 4) * 2 + (zl + dz) % 2 for dx, dz in OFFSETS]).astype(jnp.int32)


def normal_into(act_ref, gain_ref, out_ref):
    total = jnp.zeros((1, TOK), jnp.float32)
    for t in range(N_T):
        v = act_ref[t, 0].astype(jnp.float32)
        total = total + jnp.sum(v * v, axis=0, keepdims=True)
    scale = lax.rsqrt(total / D + EPS)
    for t in range(N_T):
        v = act_ref[t, 0].astype(jnp.float32)
        out_ref[t * F : (t + 1) * F, :] = ((v * scale) * gain_ref[t * F : (t + 1) * F, :]).astype(jnp.bfloat16)
    return scale


def inner_kernel(place, *refs):
    w = refs[:N_DP]
    saved, dy, gain, weight, dg_out, dgs_out, scale_out, stat_out, normal = refs[N_DP:]
    scale = normal_into(saved, gain, normal)
    scale_out[...] = scale
    row = weight[...]
    stat = jnp.zeros((1, TOK), jnp.float32)
    step = 112
    for m in range(0, G, step):
        gate = jnp.zeros((step, TOK), jnp.float32)
        up = jnp.zeros((step, TOK), jnp.float32)
        hid = jnp.zeros((step, TOK), jnp.float32)
        for r in range(N_DP):
            d = place[r]
            n = normal[pl.ds(pl.multiple_of(d * DS, DS), DS), :]
            g = dy[pl.ds(2 * d, 2), 0].reshape(DS, TOK)
            gate = gate + jnp.dot(w[r][m : m + step, :], n, preferred_element_type=jnp.float32)
            up = up + jnp.dot(w[r][G + m : G + m + step, :], n, preferred_element_type=jnp.float32)
            hid = hid + jnp.dot(w[r][2 * G + m : 2 * G + m + step, :], g, preferred_element_type=jnp.float32)
        sg = jax.nn.sigmoid(gate)
        hid = hid * row
        dgate = hid * up * (sg * (1.0 + gate * (1.0 - sg)))
        dup = hid * (gate * sg)
        dgate_r, dup_r = dgate.astype(jnp.bfloat16), dup.astype(jnp.bfloat16)
        dg_out[m : m + step, :] = dgate_r
        dg_out[G + m : G + m + step, :] = dup_r
        dgs_out[m : m + step, :] = (dgate * scale).astype(jnp.bfloat16)
        dgs_out[G + m : G + m + step, :] = (dup * scale).astype(jnp.bfloat16)
        stat = stat + jnp.sum(
            dgate_r.astype(jnp.float32) * gate + dup_r.astype(jnp.float32) * up, axis=0, keepdims=True
        )
    stat_out[...] = stat


def outer_kernel(place, *refs):
    w = refs[:N_DP]
    dg, act, gain, weight, stat, out, normal, hidden, dg_t, hid_t = refs[N_DP:]
    normal_into(act, gain, normal)
    row = weight[...]
    step = 112
    for m in range(0, G, step):
        gate = jnp.zeros((step, TOK), jnp.float32)
        up = jnp.zeros((step, TOK), jnp.float32)
        for r in range(N_DP):
            n = normal[pl.ds(pl.multiple_of(place[r] * DS, DS), DS), :]
            gate = gate + jnp.dot(w[r][m : m + step, :], n, preferred_element_type=jnp.float32)
            up = up + jnp.dot(w[r][G + m : G + m + step, :], n, preferred_element_type=jnp.float32)
        hidden[m : m + step, :] = gate * jax.nn.sigmoid(gate) * up * row
    dg_t[...] = dg[...].astype(jnp.float32).T.astype(jnp.bfloat16)
    hid_t[...] = hidden[...].T.astype(jnp.bfloat16)
    for r in range(N_DP):
        at = pl.ds(2 * place[r], 2)
        into = jnp.dot(dg_t[...], w[r][: 2 * G, :], preferred_element_type=jnp.float32)
        out[at, 0:F, :] = into.T.astype(jnp.bfloat16).reshape(2, F, TOK)
        part = jnp.dot(hid_t[...], w[r][2 * G :, :], preferred_element_type=jnp.float32)
        out[at, F : 2 * F, :] = part.T.astype(jnp.bfloat16).reshape(2, F, TOK)
    me = place[N_DP]
    value = stat[...]
    high = value.astype(jnp.bfloat16).astype(jnp.float32)
    rows = lax.broadcasted_iota(jnp.int32, (2 * N_T, TOK), 0)
    block = jnp.where(rows == me, high, jnp.where(rows == me + N_T, value - high, 0.0)).astype(jnp.bfloat16)
    for t in range(N_T):
        out[t, 2 * F :, :] = block


def grad_kernel(place, *refs):
    dgs = refs[:N_DP]
    near, far, gain, near_out, far_out = refs[N_DP:]
    own = place[0]
    opposite = lax.rem(own + 4, N_DP)
    step = 336
    for src, at, out in ((near, own, near_out), (far, opposite, far_out)):
        lanes = gain[:, pl.ds(pl.multiple_of(at * DS, DS), DS)]
        for m in range(0, 2 * G, step):
            total = jnp.zeros((step, DS), jnp.float32)
            for r in range(N_DP):
                v = src[pl.ds(2 * place[r], 2), 0].reshape(DS, TOK)
                total = total + lax.dot_general(
                    dgs[r][m : m + step, :], v, (((1,), (1,)), ((), ())), preferred_element_type=jnp.float32
                )
            out[m : m + step, :] = (total * lanes).astype(jnp.bfloat16)


def assemble_kernel(place, *refs):
    parts = refs[:N_DP]
    gate_out, up_out, sems = refs[N_DP:]
    copies = []
    for r in range(N_DP):
        lanes = pl.ds(pl.multiple_of(place[r] * DS, DS), DS)
        copies.append(pltpu.make_async_copy(parts[r].at[:G, :], gate_out.at[:, lanes], sems.at[2 * r]))
        copies.append(pltpu.make_async_copy(parts[r].at[G:, :], up_out.at[:, lanes], sems.at[2 * r + 1]))
    for copy in copies:
        copy.start()
    for copy in copies:
        copy.wait()


def params():
    return pltpu.CompilerParams(vmem_limit_bytes=VMEM_LIMIT)


def cost(flops, nbytes):
    return pl.CostEstimate(flops=flops, bytes_accessed=nbytes, transcendentals=0)


def of(array, k):
    return pl.BlockSpec((N_T, 1, F, TOK), lambda *_: (0, k, 0, 0), memory_space=pltpu.VMEM)


def combine(route_ids, probs):
    return jnp.sum(jnp.where(route_ids == 0, probs, jnp.zeros_like(probs)), axis=-1)[None, :]


def local(
    passed_activations,
    kept_section_input,
    handed_grads,
    norm_gain,
    gate_weight,
    up_weight,
    down_weight,
    routes,
    route_probs,
):
    place = places()
    here = lax.axis_index("y") * 2 + lax.axis_index("c")
    place_t = jnp.concatenate([place, here[None].astype(jnp.int32)])
    saved_t = kept_section_input[0].T
    acts_t = shift(passed_activations[0].T, s=1)
    dy_t = shift(handed_grads[0].T, s=-1)
    near = swapped(saved_t, 0)
    far = swapped(saved_t, 2)
    weights = gather_ring(jnp.concatenate([gate_weight[0].T, up_weight[0].T, down_weight[0]], axis=0))
    acts = lax.all_gather(
        jnp.concatenate([acts_t, dy_t, saved_t, near, far], axis=0), ("y", "c"), axis=0
    ).reshape(N_T, 5, F, TOK)
    gain = norm_gain[0]
    gain_col = gain[:, None]
    weight_f = combine(routes[0, 0], route_probs[0, 0])
    weight_b = combine(routes[0, 1], route_probs[0, 1])

    bf, f32 = jnp.bfloat16, jnp.float32
    dg, dgs, scale_b, stat = pl.pallas_call(
        inner_kernel,
        grid=(1,),
        in_specs=[SM] + [VM] * N_DP + [of(acts, 2), of(acts, 1), VM, VM],
        out_specs=[VM] * 4,
        out_shape=[
            jax.ShapeDtypeStruct((2 * G, TOK), bf),
            jax.ShapeDtypeStruct((2 * G, TOK), bf),
            jax.ShapeDtypeStruct((1, TOK), f32),
            jax.ShapeDtypeStruct((1, TOK), f32),
        ],
        scratch_shapes=[pltpu.VMEM((D, TOK), bf)],
        compiler_params=params(),
        cost_estimate=cost(6 * D * G * TOK, 12 << 20),
        name="inner",
    )(place, *weights, acts, acts, gain_col, weight_b)
    dgs_all = gather_ring(dgs)
    payload = pl.pallas_call(
        outer_kernel,
        grid=(1,),
        in_specs=[SM] + [VM] * N_DP + [VM, of(acts, 0), VM, VM, VM],
        out_specs=VM,
        out_shape=jax.ShapeDtypeStruct((N_T, 2 * F + 2 * N_T, TOK), bf),
        scratch_shapes=[
            pltpu.VMEM((D, TOK), bf),
            pltpu.VMEM((G, TOK), f32),
            pltpu.VMEM((TOK, 2 * G), bf),
            pltpu.VMEM((TOK, G), bf),
        ],
        compiler_params=params(),
        cost_estimate=cost(10 * D * G * TOK, 12 << 20),
        name="outer",
    )(place_t, *weights, dg, acts, gain_col, weight_f, stat)
    summed = lax.psum_scatter(payload, ("y", "c"), scatter_dimension=0)

    near_grad, far_grad = pl.pallas_call(
        grad_kernel,
        grid=(1,),
        in_specs=[SM] + [VM] * N_DP + [of(acts, 3), of(acts, 4), VM],
        out_specs=[VM, VM],
        out_shape=[jax.ShapeDtypeStruct((2 * G, DS), bf)] * 2,
        compiler_params=params(),
        cost_estimate=cost(8 * DS * G * TOK * N_DP, 8 << 20),
        name="grad",
    )(place, *dgs_all, acts, acts, gain[None, :])
    z = shift(near_grad, zl=1)
    behind = shift(near_grad, x=1)
    ahead = shift(near_grad, x=-1)
    z_far = shift(far_grad, zl=1)
    z_behind = shift(z, x=1)
    z_ahead = shift(z, x=-1)
    parts = [near_grad, z, behind, ahead, z_behind, z_ahead, far_grad, z_far]
    grad_g, grad_u = pl.pallas_call(
        assemble_kernel,
        in_specs=[SM] + [HB] * N_DP,
        out_specs=[HB, HB],
        out_shape=[jax.ShapeDtypeStruct((G, D), bf)] * 2,
        scratch_shapes=[pltpu.SemaphoreType.DMA((2 * N_DP,))],
        compiler_params=params(),
        cost_estimate=cost(0, 8 << 20),
        name="assemble",
    )(place, *parts)

    into = summed[:F].astype(f32)
    mean_stat = jnp.sum(summed[2 * F :].astype(f32), axis=0, keepdims=True) / D
    gain_here = lax.dynamic_slice_in_dim(gain, here * F, F)[:, None]
    output = (acts_t.astype(f32) + summed[F : 2 * F].astype(f32)).astype(bf)
    hat = saved_t.astype(f32) * scale_b
    stored = (dy_t.astype(f32) + scale_b * (into * gain_here - hat * mean_stat)).astype(bf)
    return (output.T[None], stored.T[None], grad_g.T[None], grad_u.T[None])


def solution(mesh):
    fine = Mesh(mesh.devices.reshape(tuple(SIZES[a] for a in AXES)), AXES)
    dp, tensor = ("x", "zl"), ("y", "c")
    placed = (
        P("s", dp, tensor),
        P("s", dp, tensor),
        P("s", dp, tensor),
        P("s", None),
        P("s", dp, tensor),
        P("s", dp, tensor),
        P("s", tensor, dp),
        P("s", None, dp, None),
        P("s", None, dp, None),
    )
    return jax.shard_map(
        local,
        mesh=fine,
        in_specs=placed,
        out_specs=(
            P("s", dp, tensor),
            P("s", dp, tensor),
            P("s", None, tensor),
            P("s", None, tensor),
        ),
        check_vma=False,
    )
```

```python
import jax
import jax.numpy as jnp
import numpy as np
from jax import lax
from jax.experimental import pallas as pl
from jax.experimental.pallas import tpu as pltpu
from jax.sharding import Mesh, PartitionSpec as P

EPS = 1e-05
AXES = ("x", "zl", "s", "y", "c")
SIZES = {"x": 4, "zl": 2, "s": 4, "y": 8, "c": 2}
D = 3072
TOK = 256
G = 336
F = 192
N_T = 16
N_DP = 8
DS = D // N_DP
N_EARLY = 6
TILE = 112
OFFSETS = ((0, 0), (0, 1), (-1, 0), (1, 0), (-1, 1), (1, 1), (2, 0), (2, 1))

VM = pl.BlockSpec(memory_space=pltpu.VMEM)
HB = pl.BlockSpec(memory_space=pl.ANY)
SM = pl.BlockSpec(memory_space=pltpu.SMEM)


def shift(value, **steps):
    axes = tuple(a for a in AXES if a in steps)
    sizes = [SIZES[a] for a in axes]
    pairs = []
    for i in range(int(np.prod(sizes))):
        at = np.unravel_index(i, sizes)
        to = [(at[k] + steps[a]) % sizes[k] for k, a in enumerate(axes)]
        pairs.append((i, int(np.ravel_multi_index(to, sizes))))
    return lax.ppermute(value, axes if len(axes) > 1 else axes[0], pairs)


def swapped(value, step):
    pairs = []
    for e in range(N_DP):
        for y in range(N_DP):
            d = (((y // 2) + step) % 4) * 2 + y % 2
            pairs.append((e * N_DP + y, d * N_DP + e))
    return lax.ppermute(value, ("x", "zl", "y"), pairs)


def gather_ring(own, rider=None):
    z = shift(own, zl=1)
    behind = shift(own, x=1)
    ahead = shift(own, x=-1)
    z, behind, ahead = lax.optimization_barrier((z, behind, ahead))
    z_behind = shift(z, x=1)
    z_ahead = shift(z, x=-1)
    riders = ()
    if rider is not None:
        riders = tuple(rider(z))
        z_behind, z_ahead, *riders = lax.optimization_barrier((z_behind, z_ahead, *riders))
    across = shift(behind, x=1)
    z_across = shift(z_ahead, x=-1)
    return [own, z, behind, ahead, z_behind, z_ahead, across, z_across], riders


def after(value, earlier):
    return lax.optimization_barrier((value, earlier))[0]


def places():
    x, zl = lax.axis_index("x"), lax.axis_index("zl")
    return jnp.stack([((x + dx) % 4) * 2 + (zl + dz) % 2 for dx, dz in OFFSETS]).astype(jnp.int32)


def normal_into(act_ref, gain_ref, out_ref):
    total = jnp.zeros((1, TOK), jnp.float32)
    for t in range(N_T):
        v = act_ref[t].astype(jnp.float32)
        total = total + jnp.sum(v * v, axis=0, keepdims=True)
    scale = lax.rsqrt(total / D + EPS)
    for t in range(N_T):
        v = act_ref[t].astype(jnp.float32)
        out_ref[t * F : (t + 1) * F, :] = ((v * scale) * gain_ref[t * F : (t + 1) * F, :]).astype(jnp.bfloat16)
    return scale


def fetch(pairs, sems):
    copies = [pltpu.make_async_copy(src, dst, sems.at[i]) for i, (src, dst) in enumerate(pairs)]
    for copy in copies:
        copy.start()
    return copies


def early_kernel(place, *refs):
    w_from = refs[:N_EARLY]
    acts, gain, b_out, f_out, nb_out, nf_out, scale_out, saved, dy, act, w, normal_b, normal_f, sems = refs[N_EARLY:]
    copies = fetch(
        [(acts.at[:, 2], saved), (acts.at[:, 0], act), (acts.at[:, 1], dy)]
        + [(w_from[r], w.at[r]) for r in range(N_EARLY)],
        sems,
    )
    copies[0].wait()
    scale_out[...] = normal_into(saved, gain, normal_b)
    copies[1].wait()
    normal_into(act, gain, normal_f)
    for copy in copies[2:]:
        copy.wait()
    for i in range(N_DP - N_EARLY):
        rows = pl.ds(pl.multiple_of(place[N_EARLY + i] * DS, DS), DS)
        nb_out[i] = normal_b[rows, :]
        nf_out[i] = normal_f[rows, :]
    for m in range(0, G, TILE):
        sums = [jnp.zeros((TILE, TOK), jnp.float32) for _ in range(5)]
        for r in range(N_EARLY):
            d = place[r]
            rows = pl.ds(pl.multiple_of(d * DS, DS), DS)
            n, f = normal_b[rows, :], normal_f[rows, :]
            g = dy[pl.ds(2 * d, 2)].reshape(DS, TOK)
            w_g = w[r, m : m + TILE, :]
            w_u = w[r, G + m : G + m + TILE, :]
            w_d = w[r, 2 * G + m : 2 * G + m + TILE, :]
            for k, (left, right) in enumerate(((w_g, n), (w_u, n), (w_d, g), (w_g, f), (w_u, f))):
                sums[k] = sums[k] + jnp.dot(left, right, preferred_element_type=jnp.float32)
        for k in range(3):
            b_out[k * G + m : k * G + m + TILE, :] = sums[k]
        for k in range(2):
            f_out[k * G + m : k * G + m + TILE, :] = sums[3 + k]


def inner_kernel(place, w_6, w_7, early, normal, acts, weight, scale_ref, dg_out, dgs_out, stat_out, dy, sems):
    w = (w_6, w_7)
    copies = fetch([(acts.at[pl.ds(2 * place[N_EARLY + i], 2), 1], dy.at[i]) for i in range(N_DP - N_EARLY)], sems)
    for copy in copies:
        copy.wait()
    scale = scale_ref[...]
    row = weight[...]
    stat = jnp.zeros((1, TOK), jnp.float32)
    for m in range(0, G, TILE):
        gate, up, hid = (early[k * G + m : k * G + m + TILE, :] for k in range(3))
        for i in range(N_DP - N_EARLY):
            n, g = normal[i], dy[i].reshape(DS, TOK)
            gate = gate + jnp.dot(w[i][m : m + TILE, :], n, preferred_element_type=jnp.float32)
            up = up + jnp.dot(w[i][G + m : G + m + TILE, :], n, preferred_element_type=jnp.float32)
            hid = hid + jnp.dot(w[i][2 * G + m : 2 * G + m + TILE, :], g, preferred_element_type=jnp.float32)
        sg = jax.nn.sigmoid(gate)
        hid = hid * row
        dgate = hid * up * (sg * (1.0 + gate * (1.0 - sg)))
        dup = hid * (gate * sg)
        dgate_r, dup_r = dgate.astype(jnp.bfloat16), dup.astype(jnp.bfloat16)
        dg_out[m : m + TILE, :] = dgate_r
        dg_out[G + m : G + m + TILE, :] = dup_r
        dgs_out[m : m + TILE, :] = (dgate * scale).astype(jnp.bfloat16)
        dgs_out[G + m : G + m + TILE, :] = (dup * scale).astype(jnp.bfloat16)
        stat = stat + jnp.sum(
            dgate_r.astype(jnp.float32) * gate + dup_r.astype(jnp.float32) * up, axis=0, keepdims=True
        )
    stat_out[...] = stat


def outer_kernel(place, *refs):
    w_from = refs[:N_DP]
    dg, early, normal, weight, stat, out, w, hidden, dg_t, hid_t, sems = refs[N_DP:]
    order = list(range(N_EARLY, N_DP)) + list(range(N_EARLY))
    copies = fetch([(w_from[r], w.at[r]) for r in order], sems)
    dg_t[...] = dg[...].astype(jnp.float32).T.astype(jnp.bfloat16)
    row = weight[...]
    last = N_DP - N_EARLY
    for copy in copies[:last]:
        copy.wait()
    for m in range(0, G, TILE):
        gate, up = (early[k * G + m : k * G + m + TILE, :] for k in range(2))
        for i in range(last):
            n = normal[i]
            gate = gate + jnp.dot(w[N_EARLY + i, m : m + TILE, :], n, preferred_element_type=jnp.float32)
            up = up + jnp.dot(w[N_EARLY + i, G + m : G + m + TILE, :], n, preferred_element_type=jnp.float32)
        hidden[m : m + TILE, :] = gate * jax.nn.sigmoid(gate) * up * row
    hid_t[...] = hidden[...].T.astype(jnp.bfloat16)
    for k, r in enumerate(order):
        if k >= last:
            copies[k].wait()
        at = pl.ds(2 * place[r], 2)
        into = jnp.dot(dg_t[...], w[r, : 2 * G, :], preferred_element_type=jnp.float32)
        out[at, 0:F, :] = into.T.astype(jnp.bfloat16).reshape(2, F, TOK)
        part = jnp.dot(hid_t[...], w[r, 2 * G :, :], preferred_element_type=jnp.float32)
        out[at, F : 2 * F, :] = part.T.astype(jnp.bfloat16).reshape(2, F, TOK)
    me = place[N_DP]
    value = stat[...]
    high = value.astype(jnp.bfloat16).astype(jnp.float32)
    rows = lax.broadcasted_iota(jnp.int32, (2 * N_T, TOK), 0)
    block = jnp.where(rows == me, high, jnp.where(rows == me + N_T, value - high, 0.0)).astype(jnp.bfloat16)
    for t in range(N_T):
        out[t, 2 * F :, :] = block


def grad_kernel(place, *refs):
    dgs = refs[:N_DP]
    near, far, gain, near_out, far_out = refs[N_DP:]
    own = place[0]
    opposite = lax.rem(own + 4, N_DP)
    step = 336
    for src, at, out in ((near, own, near_out), (far, opposite, far_out)):
        lanes = gain[:, pl.ds(pl.multiple_of(at * DS, DS), DS)]
        for m in range(0, 2 * G, step):
            total = jnp.zeros((step, DS), jnp.float32)
            for r in range(N_DP):
                v = src[pl.ds(2 * place[r], 2), 0].reshape(DS, TOK)
                total = total + lax.dot_general(
                    dgs[r][m : m + step, :], v, (((1,), (1,)), ((), ())), preferred_element_type=jnp.float32
                )
            out[m : m + step, :] = (total * lanes).astype(jnp.bfloat16)


def assemble_kernel(place, *refs):
    parts = refs[:N_DP]
    gate_out, up_out = refs[N_DP:]
    for r in range(N_DP):
        lanes = pl.ds(pl.multiple_of(place[r] * DS, DS), DS)
        gate_out[:, lanes] = parts[r][:G, :]
        up_out[:, lanes] = parts[r][G:, :]


def params(mib):
    return pltpu.CompilerParams(vmem_limit_bytes=mib << 20)


def cost(flops, nbytes):
    return pl.CostEstimate(flops=flops, bytes_accessed=nbytes, transcendentals=0)


def of(array, k):
    return pl.BlockSpec((N_T, 1, F, TOK), lambda *_: (0, k, 0, 0), memory_space=pltpu.VMEM)


def combine(route_ids, probs):
    return jnp.sum(jnp.where(route_ids == 0, probs, jnp.zeros_like(probs)), axis=-1)[None, :]


def local(
    passed_activations,
    kept_section_input,
    handed_grads,
    norm_gain,
    gate_weight,
    up_weight,
    down_weight,
    routes,
    route_probs,
):
    place = places()
    here = lax.axis_index("y") * 2 + lax.axis_index("c")
    place_t = jnp.concatenate([place, here[None].astype(jnp.int32)])
    saved_t = kept_section_input[0].T
    acts_t = shift(passed_activations[0].T, s=1)
    dy_t = shift(handed_grads[0].T, s=-1)
    own_weights = jnp.concatenate([gate_weight[0].T, up_weight[0].T, down_weight[0]], axis=0)

    def swaps(first):
        block = after(saved_t, first)
        return swapped(block, 0), swapped(block, 2)

    weights, (near, far) = gather_ring(own_weights, swaps)
    acts = lax.all_gather(
        after(jnp.concatenate([acts_t, dy_t, saved_t], axis=0), own_weights), ("y", "c"), axis=0
    ).reshape(N_T, 3, F, TOK)
    far_tokens = lax.all_gather(jnp.concatenate([near, far], axis=0), ("y", "c"), axis=0).reshape(N_T, 2, F, TOK)
    gain = norm_gain[0]
    gain_col = gain[:, None]
    weight_f = combine(routes[0, 0], route_probs[0, 0])
    weight_b = combine(routes[0, 1], route_probs[0, 1])

    bf, f32 = jnp.bfloat16, jnp.float32
    last = N_DP - N_EARLY
    early_b, early_f, normal_b, normal_f, scale_b = pl.pallas_call(
        early_kernel,
        in_specs=[SM] + [HB] * N_EARLY + [HB, VM],
        out_specs=[VM] * 5,
        out_shape=[
            jax.ShapeDtypeStruct((3 * G, TOK), f32),
            jax.ShapeDtypeStruct((2 * G, TOK), f32),
            jax.ShapeDtypeStruct((last, DS, TOK), bf),
            jax.ShapeDtypeStruct((last, DS, TOK), bf),
            jax.ShapeDtypeStruct((1, TOK), f32),
        ],
        scratch_shapes=[
            pltpu.VMEM((N_T, F, TOK), bf),
            pltpu.VMEM((N_T, F, TOK), bf),
            pltpu.VMEM((N_T, F, TOK), bf),
            pltpu.VMEM((N_EARLY, 3 * G, DS), bf),
            pltpu.VMEM((D, TOK), bf),
            pltpu.VMEM((D, TOK), bf),
            pltpu.SemaphoreType.DMA((N_EARLY + 3,)),
        ],
        compiler_params=params(56),
        cost_estimate=cost(10 * D * G * TOK, 32 << 20),
        name="early",
    )(place, *weights[:N_EARLY], acts, gain_col)
    dg, dgs, stat = pl.pallas_call(
        inner_kernel,
        in_specs=[SM] + [VM] * 4 + [HB, VM, VM],
        out_specs=[VM] * 3,
        out_shape=[
            jax.ShapeDtypeStruct((2 * G, TOK), bf),
            jax.ShapeDtypeStruct((2 * G, TOK), bf),
            jax.ShapeDtypeStruct((1, TOK), f32),
        ],
        scratch_shapes=[pltpu.VMEM((last, 2, F, TOK), bf), pltpu.SemaphoreType.DMA((last,))],
        compiler_params=params(32),
        cost_estimate=cost(2 * D * G * TOK, 12 << 20),
        name="inner",
    )(place, *weights[N_EARLY:], early_b, normal_b, acts, weight_b, scale_b)
    dgs_all, _ = gather_ring(dgs)
    payload = pl.pallas_call(
        outer_kernel,
        in_specs=[SM] + [HB] * N_DP + [VM] * 5,
        out_specs=VM,
        out_shape=jax.ShapeDtypeStruct((N_T, 2 * F + 2 * N_T, TOK), bf),
        scratch_shapes=[
            pltpu.VMEM((N_DP, 3 * G, DS), bf),
            pltpu.VMEM((G, TOK), f32),
            pltpu.VMEM((TOK, 2 * G), bf),
            pltpu.VMEM((TOK, G), bf),
            pltpu.SemaphoreType.DMA((N_DP,)),
        ],
        compiler_params=params(56),
        cost_estimate=cost(8 * D * G * TOK, 28 << 20),
        name="outer",
    )(place_t, *weights, dg, early_f, normal_f, weight_f, stat)
    payload = after(payload, tuple(dgs_all[1:4]))
    summed = lax.psum_scatter(payload, ("y", "c"), scatter_dimension=0)

    near_grad, far_grad = pl.pallas_call(
        grad_kernel,
        grid=(1,),
        in_specs=[SM] + [VM] * N_DP + [of(far_tokens, 0), of(far_tokens, 1), VM],
        out_specs=[VM, VM],
        out_shape=[jax.ShapeDtypeStruct((2 * G, DS), bf)] * 2,
        compiler_params=params(24),
        cost_estimate=cost(8 * DS * G * TOK * N_DP, 8 << 20),
        name="grad",
    )(place, *dgs_all, far_tokens, far_tokens, gain[None, :])
    z = shift(near_grad, zl=1)
    behind = shift(near_grad, x=1)
    ahead = shift(near_grad, x=-1)
    z_far = shift(far_grad, zl=1)
    z_behind = shift(z, x=1)
    z_ahead = shift(z, x=-1)
    parts = [near_grad, z, behind, ahead, z_behind, z_ahead, far_grad, z_far]
    grad_g, grad_u = pl.pallas_call(
        assemble_kernel,
        in_specs=[SM] + [VM] * N_DP,
        out_specs=[VM, VM],
        out_shape=[jax.ShapeDtypeStruct((G, D), bf)] * 2,
        compiler_params=params(24),
        cost_estimate=cost(0, 8 << 20),
        name="assemble",
    )(place, *parts)

    into = summed[:F].astype(f32)
    mean_stat = jnp.sum(summed[2 * F :].astype(f32), axis=0, keepdims=True) / D
    gain_here = lax.dynamic_slice_in_dim(gain, here * F, F)[:, None]
    output = (acts_t.astype(f32) + summed[F : 2 * F].astype(f32)).astype(bf)
    hat = saved_t.astype(f32) * scale_b
    stored = (dy_t.astype(f32) + scale_b * (into * gain_here - hat * mean_stat)).astype(bf)
    return (output.T[None], stored.T[None], grad_g.T[None], grad_u.T[None])


def solution(mesh):
    fine = Mesh(mesh.devices.reshape(tuple(SIZES[a] for a in AXES)), AXES)
    dp, tensor = ("x", "zl"), ("y", "c")
    placed = (
        P("s", dp, tensor),
        P("s", dp, tensor),
        P("s", dp, tensor),
        P("s", None),
        P("s", dp, tensor),
        P("s", dp, tensor),
        P("s", tensor, dp),
        P("s", None, dp, None),
        P("s", None, dp, None),
    )
    return jax.shard_map(
        local,
        mesh=fine,
        in_specs=placed,
        out_specs=(
            P("s", dp, tensor),
            P("s", dp, tensor),
            P("s", None, tensor),
            P("s", None, tensor),
        ),
        check_vma=False,
    )
```

```python
import jax
import jax.numpy as jnp
import numpy as np
from jax import lax
from jax.experimental import pallas as pl
from jax.experimental.pallas import tpu as pltpu
from jax.sharding import Mesh, PartitionSpec as P

EPS = 1e-05
AXES = ("x", "zl", "s", "y", "c")
SIZES = {"x": 4, "zl": 2, "s": 4, "y": 8, "c": 2}
D = 3072
TOK = 256
G = 336
F = 192
N_T = 16
N_DP = 8
DS = D // N_DP
N_EARLY = 7
CUT = 512
TILE = 112
OFFSETS = ((0, 0), (0, 1), (-1, 0), (1, 0), (-1, 1), (1, 1), (2, 0), (2, 1))

VM = pl.BlockSpec(memory_space=pltpu.VMEM)
HB = pl.BlockSpec(memory_space=pl.ANY)
SM = pl.BlockSpec(memory_space=pltpu.SMEM)


def shift(value, **steps):
    axes = tuple(a for a in AXES if a in steps)
    sizes = [SIZES[a] for a in axes]
    pairs = []
    for i in range(int(np.prod(sizes))):
        at = np.unravel_index(i, sizes)
        to = [(at[k] + steps[a]) % sizes[k] for k, a in enumerate(axes)]
        pairs.append((i, int(np.ravel_multi_index(to, sizes))))
    return lax.ppermute(value, axes if len(axes) > 1 else axes[0], pairs)


def swapped(value, step):
    pairs = []
    for e in range(N_DP):
        for y in range(N_DP):
            d = (((y // 2) + step) % 4) * 2 + y % 2
            pairs.append((e * N_DP + y, d * N_DP + e))
    return lax.ppermute(value, ("x", "zl", "y"), pairs)


def gather_ring(own):
    first = shift(own, zl=1)
    behind = shift(own, x=1)
    ahead = shift(own, x=-1)
    z, behind, ahead = lax.optimization_barrier((first, behind, ahead))
    z_behind = shift(z, x=1)
    z_ahead = shift(z, x=-1)
    across = shift(behind, x=1)
    z_across = shift(z_ahead, x=-1)
    return [own, z, behind, ahead, z_behind, z_ahead, across, z_across], first


def gather_weights(own, block, ready):
    z = shift(own, zl=1)
    behind = shift(own, x=1)
    ahead = shift(own, x=-1)
    z, behind, ahead, block, ready = lax.optimization_barrier((z, behind, ahead, block, ready))
    z_behind = shift(z, x=1)
    across = shift(ahead, x=-1)
    z_ahead = shift(ahead, zl=1)
    near, far = swapped(block, 0), swapped(block, 2)
    z_behind, across, z_ahead, near, far = lax.optimization_barrier((z_behind, across, z_ahead, near, far))
    top = shift(z_behind[:CUT], x=1)
    bottom = shift(z_ahead[CUT:], x=-1)
    return [own, z, behind, ahead, z_behind, z_ahead, across], (top, bottom), (near, far), ready


def after(value, earlier):
    return lax.optimization_barrier((value, earlier))[0]


def places():
    x, zl = lax.axis_index("x"), lax.axis_index("zl")
    return jnp.stack([((x + dx) % 4) * 2 + (zl + dz) % 2 for dx, dz in OFFSETS]).astype(jnp.int32)


def gained_into(act_ref, gain_ref, out_ref):
    total = jnp.zeros((8, TOK), jnp.float32)
    for t in range(N_T):
        v = act_ref[t].astype(jnp.float32)
        total = total + jnp.sum((v * v).reshape(F // 8, 8, TOK), axis=0)
        out_ref[t * F : (t + 1) * F, :] = (v * gain_ref[t * F : (t + 1) * F, :]).astype(jnp.bfloat16)
    return lax.rsqrt(jnp.sum(total, axis=0, keepdims=True) / D + EPS)


def fetch(pairs, sems):
    copies = [pltpu.make_async_copy(src, dst, sems.at[i]) for i, (src, dst) in enumerate(pairs)]
    for copy in copies:
        copy.start()
    return copies


def early_kernel(place, *refs):
    w_from = refs[:N_EARLY]
    acts, gain, b_out, f_out, nb_out, nf_out, scales_out, saved, dy, act, w, normal_b, normal_f, sems = refs[N_EARLY:]
    copies = fetch(
        [(acts.at[:, 2], saved), (acts.at[:, 0], act), (acts.at[:, 1], dy)]
        + [(w_from[r], w.at[r]) for r in range(N_EARLY)],
        sems,
    )
    copies[0].wait()
    scales_out[0:1, :] = gained_into(saved, gain, normal_b)
    copies[1].wait()
    scales_out[1:2, :] = gained_into(act, gain, normal_f)
    for copy in copies[2:]:
        copy.wait()
    rows = pl.ds(pl.multiple_of(place[N_EARLY] * DS, DS), DS)
    nb_out[...] = normal_b[rows, :]
    nf_out[...] = normal_f[rows, :]
    for m in range(0, G, TILE):
        sums = [jnp.zeros((TILE, TOK), jnp.float32) for _ in range(5)]
        for r in range(N_EARLY):
            d = place[r]
            rows = pl.ds(pl.multiple_of(d * DS, DS), DS)
            n, f = normal_b[rows, :], normal_f[rows, :]
            g = dy[pl.ds(2 * d, 2)].reshape(DS, TOK)
            w_g = w[r, m : m + TILE, :]
            w_u = w[r, G + m : G + m + TILE, :]
            w_d = w[r, 2 * G + m : 2 * G + m + TILE, :]
            for k, (left, right) in enumerate(((w_g, n), (w_u, n), (w_d, g), (w_g, f), (w_u, f))):
                sums[k] = sums[k] + jnp.dot(left, right, preferred_element_type=jnp.float32)
        for k in range(3):
            b_out[k * G + m : k * G + m + TILE, :] = sums[k]
        for k in range(2):
            f_out[k * G + m : k * G + m + TILE, :] = sums[3 + k]


def inner_kernel(place, top, bottom, early_from, n_from, acts, weight, scales, dg_out, dgs_out, stat_out, w, early, normal, dy, sems):
    copies = fetch(
        [
            (n_from, normal),
            (acts.at[pl.ds(2 * place[N_EARLY], 2), 1], dy),
            (top, w.at[:CUT, :]),
            (bottom, w.at[CUT:, :]),
            (early_from, early),
        ],
        sems,
    )
    scale = scales[0:1, :]
    row = weight[...]
    stat = jnp.zeros((1, TOK), jnp.float32)
    for copy in copies:
        copy.wait()
    n, g = normal[...], dy[...].reshape(DS, TOK)
    for m in range(0, G, TILE):
        gate, up, hid = (early[k * G + m : k * G + m + TILE, :] for k in range(3))
        gate = scale * (gate + jnp.dot(w[m : m + TILE, :], n, preferred_element_type=jnp.float32))
        up = scale * (up + jnp.dot(w[G + m : G + m + TILE, :], n, preferred_element_type=jnp.float32))
        hid = hid + jnp.dot(w[2 * G + m : 2 * G + m + TILE, :], g, preferred_element_type=jnp.float32)
        sg = jax.nn.sigmoid(gate)
        hid = hid * row
        dgate = hid * up * (sg * (1.0 + gate * (1.0 - sg)))
        dup = hid * (gate * sg)
        dgate_r, dup_r = dgate.astype(jnp.bfloat16), dup.astype(jnp.bfloat16)
        dg_out[m : m + TILE, :] = dgate_r
        dg_out[G + m : G + m + TILE, :] = dup_r
        dgs_out[m : m + TILE, :] = (dgate * scale).astype(jnp.bfloat16)
        dgs_out[G + m : G + m + TILE, :] = (dup * scale).astype(jnp.bfloat16)
        stat = stat + jnp.sum(
            dgate_r.astype(jnp.float32) * gate + dup_r.astype(jnp.float32) * up, axis=0, keepdims=True
        )
    stat_out[...] = stat


def outer_kernel(place, *refs):
    w_from = refs[:N_EARLY]
    top, bottom, dg, early, normal, weight, scales, stat, out, w, hidden, dg_t, hid_t, sems = refs[N_EARLY:]
    order = [N_EARLY] + list(range(N_EARLY))
    pairs = [(top, w.at[N_EARLY, :CUT, :]), (bottom, w.at[N_EARLY, CUT:, :])]
    copies = fetch(pairs + [(w_from[r], w.at[r]) for r in range(N_EARLY)], sems)
    dg_t[...] = dg[...].astype(jnp.float32).T.astype(jnp.bfloat16)
    row = weight[...]
    scale = scales[1:2, :]
    copies[0].wait()
    copies[1].wait()
    n = normal[...]
    for m in range(0, G, TILE):
        gate, up = (early[k * G + m : k * G + m + TILE, :] for k in range(2))
        gate = scale * (gate + jnp.dot(w[N_EARLY, m : m + TILE, :], n, preferred_element_type=jnp.float32))
        up = scale * (up + jnp.dot(w[N_EARLY, G + m : G + m + TILE, :], n, preferred_element_type=jnp.float32))
        hidden[m : m + TILE, :] = gate * jax.nn.sigmoid(gate) * up * row
    hid_t[...] = hidden[...].T.astype(jnp.bfloat16)
    for k, r in enumerate(order):
        if k:
            copies[k + 1].wait()
        at = pl.ds(2 * place[r], 2)
        into = jnp.dot(dg_t[...], w[r, : 2 * G, :], preferred_element_type=jnp.float32)
        out[at, 0:F, :] = into.T.astype(jnp.bfloat16).reshape(2, F, TOK)
        part = jnp.dot(hid_t[...], w[r, 2 * G :, :], preferred_element_type=jnp.float32)
        out[at, F : 2 * F, :] = part.T.astype(jnp.bfloat16).reshape(2, F, TOK)
    me = place[N_DP]
    value = stat[...]
    high = value.astype(jnp.bfloat16).astype(jnp.float32)
    rows = lax.broadcasted_iota(jnp.int32, (2 * N_T, TOK), 0)
    block = jnp.where(rows == me, high, jnp.where(rows == me + N_T, value - high, 0.0)).astype(jnp.bfloat16)
    for t in range(N_T):
        out[t, 2 * F :, :] = block


def grad_kernel(place, *refs):
    dgs_from = refs[:N_DP]
    tokens, gain, near_out, far_out, near, far, dgs, sems = refs[N_DP:]
    pairs = [(dgs_from[r], dgs.at[r]) for r in range(N_DP)]
    copies = fetch([(tokens.at[:, 0], near)] + pairs + [(tokens.at[:, 1], far)], sems)
    own = place[0]
    opposite = lax.rem(own + 4, N_DP)
    for copy in copies[:-1]:
        copy.wait()
    for src, at, out in ((near, own, near_out), (far, opposite, far_out)):
        if src is far:
            copies[-1].wait()
        lanes = gain[:, pl.ds(pl.multiple_of(at * DS, DS), DS)]
        for m in range(0, 2 * G, G):
            total = jnp.zeros((G, DS), jnp.float32)
            for r in range(N_DP):
                v = src[pl.ds(2 * place[r], 2)].reshape(DS, TOK)
                total = total + lax.dot_general(
                    dgs[r, m : m + G, :], v, (((1,), (1,)), ((), ())), preferred_element_type=jnp.float32
                )
            out[m : m + G, :] = (total * lanes).astype(jnp.bfloat16)


def assemble_kernel(place, *refs):
    parts = refs[:N_DP]
    gate_out, up_out = refs[N_DP:]
    for r in range(N_DP):
        lanes = pl.ds(pl.multiple_of(place[r] * DS, DS), DS)
        gate_out[:, lanes] = parts[r][:G, :]
        up_out[:, lanes] = parts[r][G:, :]


def params(mib):
    return pltpu.CompilerParams(vmem_limit_bytes=mib << 20)


def cost(flops, nbytes):
    return pl.CostEstimate(flops=flops, bytes_accessed=nbytes, transcendentals=0)


def combine(route_ids, probs):
    return jnp.sum(jnp.where(route_ids == 0, probs, jnp.zeros_like(probs)), axis=-1)[None, :]


def local(
    passed_activations,
    kept_section_input,
    handed_grads,
    norm_gain,
    gate_weight,
    up_weight,
    down_weight,
    routes,
    route_probs,
):
    place = places()
    here = lax.axis_index("y") * 2 + lax.axis_index("c")
    place_t = jnp.concatenate([place, here[None].astype(jnp.int32)])
    saved_t = kept_section_input[0].T
    acts_t = shift(passed_activations[0].T, s=1)
    dy_t = shift(handed_grads[0].T, s=-1)
    gain = norm_gain[0]
    own_weights = jnp.concatenate([gate_weight[0].T, up_weight[0].T, down_weight[0]], axis=0)
    ready = (gain[:, None], place_t, combine(routes[0, 0], route_probs[0, 0]), combine(routes[0, 1], route_probs[0, 1]))
    weights, (top, bottom), swaps, ready = gather_weights(own_weights, saved_t, ready)
    gain_col, place, weight_f, weight_b = ready
    acts = lax.all_gather(
        after(jnp.concatenate([acts_t, dy_t, saved_t], axis=0), own_weights), ("y", "c"), axis=0
    ).reshape(N_T, 3, F, TOK)
    tokens = lax.all_gather(jnp.concatenate(swaps, axis=0), ("y", "c"), axis=0).reshape(N_T, 2, F, TOK)

    bf, f32 = jnp.bfloat16, jnp.float32
    early_b, early_f, normal_b, normal_f, scales = pl.pallas_call(
        early_kernel,
        in_specs=[SM] + [HB] * N_EARLY + [HB, VM],
        out_specs=[VM] * 5,
        out_shape=[
            jax.ShapeDtypeStruct((3 * G, TOK), f32),
            jax.ShapeDtypeStruct((2 * G, TOK), f32),
            jax.ShapeDtypeStruct((DS, TOK), bf),
            jax.ShapeDtypeStruct((DS, TOK), bf),
            jax.ShapeDtypeStruct((2, TOK), f32),
        ],
        scratch_shapes=[
            pltpu.VMEM((N_T, F, TOK), bf),
            pltpu.VMEM((N_T, F, TOK), bf),
            pltpu.VMEM((N_T, F, TOK), bf),
            pltpu.VMEM((N_EARLY, 3 * G, DS), bf),
            pltpu.VMEM((D, TOK), bf),
            pltpu.VMEM((D, TOK), bf),
            pltpu.SemaphoreType.DMA((N_EARLY + 3,)),
        ],
        compiler_params=params(56),
        cost_estimate=cost(10 * D * G * TOK, 32 << 20),
        name="early",
    )(place, *weights, acts, gain_col)
    dg, dgs, stat = pl.pallas_call(
        inner_kernel,
        in_specs=[SM] + [HB] * 5 + [VM, VM],
        out_specs=[VM] * 3,
        out_shape=[
            jax.ShapeDtypeStruct((2 * G, TOK), bf),
            jax.ShapeDtypeStruct((2 * G, TOK), bf),
            jax.ShapeDtypeStruct((1, TOK), f32),
        ],
        scratch_shapes=[
            pltpu.VMEM((3 * G, DS), bf),
            pltpu.VMEM((3 * G, TOK), f32),
            pltpu.VMEM((DS, TOK), bf),
            pltpu.VMEM((2, F, TOK), bf),
            pltpu.SemaphoreType.DMA((5,)),
        ],
        compiler_params=params(56),
        cost_estimate=cost(2 * D * G * TOK, 12 << 20),
        name="inner",
    )(place, top, bottom, early_b, normal_b, acts, weight_b, scales)
    dgs_all, dgs_z = gather_ring(dgs)
    payload = pl.pallas_call(
        outer_kernel,
        in_specs=[SM] + [HB] * (N_EARLY + 2) + [VM] * 6,
        out_specs=VM,
        out_shape=jax.ShapeDtypeStruct((N_T, 2 * F + 2 * N_T, TOK), bf),
        scratch_shapes=[
            pltpu.VMEM((N_DP, 3 * G, DS), bf),
            pltpu.VMEM((G, TOK), f32),
            pltpu.VMEM((TOK, 2 * G), bf),
            pltpu.VMEM((TOK, G), bf),
            pltpu.SemaphoreType.DMA((N_DP + 1,)),
        ],
        compiler_params=params(56),
        cost_estimate=cost(8 * D * G * TOK, 28 << 20),
        name="outer",
    )(place, *weights, top, bottom, dg, early_f, normal_f, weight_f, scales, stat)
    payload = after(payload, dgs_z)
    summed = lax.psum_scatter(payload, ("y", "c"), scatter_dimension=0)

    near_grad, far_grad = pl.pallas_call(
        grad_kernel,
        in_specs=[SM] + [HB] * (N_DP + 1) + [VM],
        out_specs=[VM, VM],
        out_shape=[jax.ShapeDtypeStruct((2 * G, DS), bf)] * 2,
        scratch_shapes=[
            pltpu.VMEM((N_T, F, TOK), bf),
            pltpu.VMEM((N_T, F, TOK), bf),
            pltpu.VMEM((N_DP, 2 * G, TOK), bf),
            pltpu.SemaphoreType.DMA((N_DP + 2,)),
        ],
        compiler_params=params(56),
        cost_estimate=cost(8 * DS * G * TOK * N_DP, 8 << 20),
        name="grad",
    )(place, *dgs_all, tokens, gain[None, :])
    z = shift(near_grad, zl=1)
    behind = shift(near_grad, x=1)
    ahead = shift(near_grad, x=-1)
    z_far = shift(far_grad, zl=1)
    z_behind = shift(z, x=1)
    z_ahead = shift(z, x=-1)
    parts = [near_grad, z, behind, ahead, z_behind, z_ahead, far_grad, z_far]
    grad_g, grad_u = pl.pallas_call(
        assemble_kernel,
        in_specs=[SM] + [VM] * N_DP,
        out_specs=[VM, VM],
        out_shape=[jax.ShapeDtypeStruct((G, D), bf)] * 2,
        compiler_params=params(24),
        cost_estimate=cost(0, 8 << 20),
        name="assemble",
    )(place, *parts)

    into = summed[:F].astype(f32)
    mean_stat = jnp.sum(summed[2 * F :].astype(f32), axis=0, keepdims=True) / D
    gain_here = lax.dynamic_slice_in_dim(gain, here * F, F)[:, None]
    output = (acts_t.astype(f32) + summed[F : 2 * F].astype(f32)).astype(bf)
    scale_b = scales[0:1]
    hat = saved_t.astype(f32) * scale_b
    stored = (dy_t.astype(f32) + scale_b * (into * gain_here - hat * mean_stat)).astype(bf)
    return (output.T[None], stored.T[None], grad_g.T[None], grad_u.T[None])


def solution(mesh):
    fine = Mesh(mesh.devices.reshape(tuple(SIZES[a] for a in AXES)), AXES)
    dp, tensor = ("x", "zl"), ("y", "c")
    placed = (
        P("s", dp, tensor),
        P("s", dp, tensor),
        P("s", dp, tensor),
        P("s", None),
        P("s", dp, tensor),
        P("s", dp, tensor),
        P("s", tensor, dp),
        P("s", None, dp, None),
        P("s", None, dp, None),
    )
    return jax.shard_map(
        local,
        mesh=fine,
        in_specs=placed,
        out_specs=(
            P("s", dp, tensor),
            P("s", dp, tensor),
            P("s", None, tensor),
            P("s", None, tensor),
        ),
        check_vma=False,
    )
```

```python
import functools

import jax
import jax.numpy as jnp
import numpy as np
from jax import lax
from jax.experimental import pallas as pl
from jax.experimental.pallas import tpu as pltpu
from jax.sharding import Mesh, PartitionSpec as P

EPS = 1e-05
AXES = ("x", "zl", "s", "y", "c")
SIZES = {"x": 4, "zl": 2, "s": 4, "y": 8, "c": 2}
D = 3072
TOK = 256
G = 336
F = 192
N_T = 16
N_DP = 8
DS = D // N_DP
N_EARLY = 6
TILE = 336
OFFSETS = ((0, 0), (0, 1), (-1, 0), (1, 0), (-1, 1), (1, 1), (2, 0), (2, 1))

VM = pl.BlockSpec(memory_space=pltpu.VMEM)
HB = pl.BlockSpec(memory_space=pl.ANY)
SM = pl.BlockSpec(memory_space=pltpu.SMEM)


def shift(value, **steps):
    axes = tuple(a for a in AXES if a in steps)
    sizes = [SIZES[a] for a in axes]
    pairs = []
    for i in range(int(np.prod(sizes))):
        at = np.unravel_index(i, sizes)
        to = [(at[k] + steps[a]) % sizes[k] for k, a in enumerate(axes)]
        pairs.append((i, int(np.ravel_multi_index(to, sizes))))
    return lax.ppermute(value, axes if len(axes) > 1 else axes[0], pairs)


def swapped(value, step):
    pairs = []
    for e in range(N_DP):
        for y in range(N_DP):
            d = (((y // 2) + step) % 4) * 2 + y % 2
            pairs.append((e * N_DP + y, d * N_DP + e))
    return lax.ppermute(value, ("x", "zl", "y"), pairs)


def gather_ring(own, ready=()):
    z = shift(own, zl=1)
    behind = shift(own, x=1)
    ahead = shift(own, x=-1)
    z, behind, ahead, ready = lax.optimization_barrier((z, behind, ahead, ready))
    z_behind = shift(z, x=1)
    z_ahead = shift(z, x=-1)
    if ready:
        z_behind, z_ahead = lax.optimization_barrier((z_behind, z_ahead))
    across = shift(behind, x=1)
    z_across = shift(z_ahead, x=-1)
    return [own, z, behind, ahead, z_behind, z_ahead, across, z_across], ready


def after(value, earlier):
    return lax.optimization_barrier((value, earlier))[0]


def places():
    x, zl = lax.axis_index("x"), lax.axis_index("zl")
    return jnp.stack([((x + dx) % 4) * 2 + (zl + dz) % 2 for dx, dz in OFFSETS]).astype(jnp.int32)


def gained_into(act_ref, gain_ref, out_ref):
    total = jnp.zeros((8, TOK), jnp.float32)
    for t in range(N_T):
        v = act_ref[t].astype(jnp.float32)
        total = total + jnp.sum((v * v).reshape(F // 8, 8, TOK), axis=0)
        out_ref[t * F : (t + 1) * F, :] = (v * gain_ref[t * F : (t + 1) * F, :]).astype(jnp.bfloat16)
    return lax.rsqrt(jnp.sum(total, axis=0, keepdims=True) / D + EPS)


def fetch(pairs, sems):
    copies = [pltpu.make_async_copy(src, dst, sems.at[i]) for i, (src, dst) in enumerate(pairs)]
    for copy in copies:
        copy.start()
    return copies


def norm_kernel(acts, gain, b_out, f_out, scales_out, saved, act, sems):
    copies = fetch([(acts.at[:, 2], saved), (acts.at[:, 0], act)], sems)
    copies[0].wait()
    scales_out[0:1, :] = gained_into(saved, gain, b_out)
    copies[1].wait()
    scales_out[1:2, :] = gained_into(act, gain, f_out)


def early_kernel(place, *refs):
    w_from = refs[:N_EARLY]
    acts, normal_b_from, normal_f_from, b_out, f_out, dy, w, normal_b, normal_f, sems = refs[N_EARLY:]
    copies = fetch(
        [(normal_b_from, normal_b), (normal_f_from, normal_f), (acts.at[:, 1], dy)]
        + [(w_from[r], w.at[r]) for r in range(N_EARLY)],
        sems,
    )
    for copy in copies:
        copy.wait()
    for m in range(0, G, TILE):
        sums = [jnp.zeros((TILE, TOK), jnp.float32) for _ in range(5)]
        for r in range(N_EARLY):
            d = place[r]
            rows = pl.ds(pl.multiple_of(d * DS, DS), DS)
            n, f = normal_b[rows, :], normal_f[rows, :]
            g = dy[pl.ds(2 * d, 2)].reshape(DS, TOK)
            w_g = w[r, m : m + TILE, :]
            w_u = w[r, G + m : G + m + TILE, :]
            w_d = w[r, 2 * G + m : 2 * G + m + TILE, :]
            for k, (left, right) in enumerate(((w_g, n), (w_u, n), (w_d, g), (w_g, f), (w_u, f))):
                sums[k] = sums[k] + jnp.dot(left, right, preferred_element_type=jnp.float32)
        for k in range(3):
            b_out[k * G + m : k * G + m + TILE, :] = sums[k]
        for k in range(2):
            f_out[k * G + m : k * G + m + TILE, :] = sums[3 + k]


def columns(place, i):
    return pl.ds(pl.multiple_of(place[N_EARLY + i] * DS, DS), DS)


def inner_kernel(place, w_6, w_7, early_from, n_from, acts, weight, scales, dg_out, dgs_out, stat_out, w, early, normal, dy, sems):
    last = N_DP - N_EARLY
    copies = fetch(
        [(n_from.at[columns(place, i), :], normal.at[i]) for i in range(last)]
        + [(acts.at[pl.ds(2 * place[N_EARLY + i], 2), 1], dy.at[i]) for i in range(last)]
        + [(w_6, w.at[0]), (w_7, w.at[1]), (early_from, early)],
        sems,
    )
    scale = scales[0:1, :]
    row = weight[...]
    stat = jnp.zeros((1, TOK), jnp.float32)
    for copy in copies:
        copy.wait()
    for m in range(0, G, TILE):
        gate, up, hid = (early[k * G + m : k * G + m + TILE, :] for k in range(3))
        for i in range(last):
            n, g = normal[i], dy[i].reshape(DS, TOK)
            gate = gate + jnp.dot(w[i, m : m + TILE, :], n, preferred_element_type=jnp.float32)
            up = up + jnp.dot(w[i, G + m : G + m + TILE, :], n, preferred_element_type=jnp.float32)
            hid = hid + jnp.dot(w[i, 2 * G + m : 2 * G + m + TILE, :], g, preferred_element_type=jnp.float32)
        gate = scale * gate
        up = scale * up
        sg = jax.nn.sigmoid(gate)
        hid = hid * row
        dgate = hid * up * (sg * (1.0 + gate * (1.0 - sg)))
        dup = hid * (gate * sg)
        dgate_r, dup_r = dgate.astype(jnp.bfloat16), dup.astype(jnp.bfloat16)
        dg_out[m : m + TILE, :] = dgate_r
        dg_out[G + m : G + m + TILE, :] = dup_r
        dgs_out[m : m + TILE, :] = (dgate * scale).astype(jnp.bfloat16)
        dgs_out[G + m : G + m + TILE, :] = (dup * scale).astype(jnp.bfloat16)
        stat = stat + jnp.sum(
            dgate_r.astype(jnp.float32) * gate + dup_r.astype(jnp.float32) * up, axis=0, keepdims=True
        )
    stat_out[...] = stat


def outer_kernel(place, *refs):
    w_from = refs[:N_DP]
    dg, early, n_from, weight, scales, stat, keep, send, w, normal, hidden, dg_t, hid_t, sems = refs[N_DP:]
    last = N_DP - N_EARLY
    order = list(range(N_EARLY, N_DP)) + list(range(N_EARLY))
    pairs = [(n_from.at[columns(place, i), :], normal.at[i]) for i in range(last)]
    copies = fetch(pairs + [(w_from[r], w.at[r]) for r in order], sems)
    dg_t[...] = dg[...].T
    row = weight[...]
    scale = scales[1:2, :]
    for copy in copies[: 2 * last]:
        copy.wait()
    for m in range(0, G, TILE):
        gate, up = (early[k * G + m : k * G + m + TILE, :] for k in range(2))
        for i in range(last):
            n = normal[i]
            gate = gate + jnp.dot(w[N_EARLY + i, m : m + TILE, :], n, preferred_element_type=jnp.float32)
            up = up + jnp.dot(w[N_EARLY + i, G + m : G + m + TILE, :], n, preferred_element_type=jnp.float32)
        gate = scale * gate
        up = scale * up
        hidden[m : m + TILE, :] = (gate * jax.nn.sigmoid(gate) * up * row).astype(jnp.bfloat16)
    hid_t[...] = hidden[...].T
    me = place[N_DP]
    first = lax.rem(me, 2) == 0
    for k, r in enumerate(order):
        if k >= last:
            copies[last + k].wait()
        into = jnp.dot(dg_t[...], w[r, : 2 * G, :], preferred_element_type=jnp.float32)
        part = jnp.dot(hid_t[...], w[r, 2 * G :, :], preferred_element_type=jnp.float32)
        for value, low in ((into, 0), (part, F)):
            value = value.astype(jnp.bfloat16).T
            one, two = value[:F], value[F:]
            keep[place[r], low : low + F, :] = jnp.where(first, one, two)
            send[place[r], low : low + F, :] = jnp.where(first, two, one)
    value = stat[...]
    high = value.astype(jnp.bfloat16).astype(jnp.float32)
    rows = lax.broadcasted_iota(jnp.int32, (2 * N_T, TOK), 0)
    block = jnp.where(rows == me, high, jnp.where(rows == me + N_T, value - high, 0.0)).astype(jnp.bfloat16)
    for y in range(N_T // 2):
        keep[y, 2 * F :, :] = block
        send[y, 2 * F :, :] = block


def grad_kernel(blocks, place, *refs):
    dgs_from = refs[: len(blocks)]
    start = blocks[0] == 0
    if start:
        tokens, near_out, far_out, near, far, dgs, sems = refs[len(blocks) :]
    else:
        tokens, gain, near_sum, far_sum, near_out, far_out, near, far, dgs, sums, sems = refs[len(blocks) :]
    copies = []
    for k, r in enumerate(blocks):
        at = pl.ds(2 * place[r], 2)
        copies += [(tokens.at[at, 0], near.at[k]), (dgs_from[k], dgs.at[k])]
    if not start:
        copies += [(near_sum, sums.at[0]), (far_sum, sums.at[1])]
    for k, r in enumerate(blocks):
        copies.append((tokens.at[pl.ds(2 * place[r], 2), 1], far.at[k]))
    copies = fetch(copies, sems)
    for copy in copies[: -len(blocks)]:
        copy.wait()
    for j, (src, out) in enumerate(((near, near_out), (far, far_out))):
        if j:
            for copy in copies[-len(blocks) :]:
                copy.wait()
        for m in range(0, 2 * G, G):
            total = jnp.zeros((G, DS), jnp.float32) if start else sums[j, m : m + G, :]
            for k in range(len(blocks)):
                v = src[k].reshape(DS, TOK)
                total = total + lax.dot_general(
                    dgs[k, m : m + G, :], v, (((1,), (1,)), ((), ())), preferred_element_type=jnp.float32
                )
            if start:
                out[m : m + G, :] = total
            else:
                at = place[0] if j == 0 else lax.rem(place[0] + 4, N_DP)
                out[m : m + G, :] = (total * gain[:, pl.ds(pl.multiple_of(at * DS, DS), DS)]).astype(jnp.bfloat16)


def assemble_kernel(place, *refs):
    parts = refs[:N_DP]
    gate_out, up_out = refs[N_DP:]
    for r in range(N_DP):
        lanes = pl.ds(pl.multiple_of(place[r] * DS, DS), DS)
        gate_out[:, lanes] = parts[r][:G, :]
        up_out[:, lanes] = parts[r][G:, :]


def params(mib):
    return pltpu.CompilerParams(vmem_limit_bytes=mib << 20)


def cost(flops, nbytes):
    return pl.CostEstimate(flops=flops, bytes_accessed=nbytes, transcendentals=0)


def combine(route_ids, probs):
    return jnp.sum(jnp.where(route_ids == 0, probs, jnp.zeros_like(probs)), axis=-1)[None, :]


def local(
    passed_activations,
    kept_section_input,
    handed_grads,
    norm_gain,
    gate_weight,
    up_weight,
    down_weight,
    routes,
    route_probs,
):
    place = places()
    here = lax.axis_index("y") * 2 + lax.axis_index("c")
    place_t = jnp.concatenate([place, here[None].astype(jnp.int32)])
    saved_t = kept_section_input[0].T
    acts_t = shift(passed_activations[0].T, s=1)
    dy_t = shift(handed_grads[0].T, s=-1)
    gain = norm_gain[0]
    own_weights = jnp.concatenate([gate_weight[0].T, up_weight[0].T, down_weight[0]], axis=0)
    ready = (gain[:, None], place_t, combine(routes[0, 0], route_probs[0, 0]), combine(routes[0, 1], route_probs[0, 1]))
    weights, ready = gather_ring(own_weights, ready)
    gain_col, place, weight_f, weight_b = ready
    acts = lax.all_gather(
        after(jnp.concatenate([acts_t, dy_t, saved_t], axis=0), own_weights), ("y", "c"), axis=0
    ).reshape(N_T, 3, F, TOK)

    bf, f32 = jnp.bfloat16, jnp.float32
    last = N_DP - N_EARLY
    normal_b, normal_f, scales = pl.pallas_call(
        norm_kernel,
        in_specs=[HB, VM],
        out_specs=[VM] * 3,
        out_shape=[
            jax.ShapeDtypeStruct((D, TOK), bf),
            jax.ShapeDtypeStruct((D, TOK), bf),
            jax.ShapeDtypeStruct((2, TOK), f32),
        ],
        scratch_shapes=[pltpu.VMEM((N_T, F, TOK), bf), pltpu.VMEM((N_T, F, TOK), bf), pltpu.SemaphoreType.DMA((2,))],
        compiler_params=params(56),
        cost_estimate=cost(8 * D * TOK, 16 << 20),
        name="norms",
    )(acts, gain_col)
    swap_t = after(saved_t, scales)
    near, far = swapped(swap_t, 0), swapped(swap_t, 2)
    early_b, early_f = pl.pallas_call(
        early_kernel,
        in_specs=[SM] + [HB] * (N_EARLY + 3),
        out_specs=[VM] * 2,
        out_shape=[jax.ShapeDtypeStruct((3 * G, TOK), f32), jax.ShapeDtypeStruct((2 * G, TOK), f32)],
        scratch_shapes=[
            pltpu.VMEM((N_T, F, TOK), bf),
            pltpu.VMEM((N_EARLY, 3 * G, DS), bf),
            pltpu.VMEM((D, TOK), bf),
            pltpu.VMEM((D, TOK), bf),
            pltpu.SemaphoreType.DMA((N_EARLY + 3,)),
        ],
        compiler_params=params(56),
        cost_estimate=cost(10 * D * G * TOK, 32 << 20),
        name="early",
    )(place, *weights[:N_EARLY], acts, normal_b, normal_f)
    near, far, early_b, *weights[N_EARLY:] = lax.optimization_barrier((near, far, early_b, *weights[N_EARLY:]))
    tokens = lax.all_gather(jnp.concatenate([near, far], axis=0), ("y", "c"), axis=0).reshape(N_T, 2, F, TOK)
    dg, dgs, stat = pl.pallas_call(
        inner_kernel,
        in_specs=[SM] + [HB] * 5 + [VM, VM],
        out_specs=[VM] * 3,
        out_shape=[
            jax.ShapeDtypeStruct((2 * G, TOK), bf),
            jax.ShapeDtypeStruct((2 * G, TOK), bf),
            jax.ShapeDtypeStruct((1, TOK), f32),
        ],
        scratch_shapes=[
            pltpu.VMEM((last, 3 * G, DS), bf),
            pltpu.VMEM((3 * G, TOK), f32),
            pltpu.VMEM((last, DS, TOK), bf),
            pltpu.VMEM((last, 2, F, TOK), bf),
            pltpu.SemaphoreType.DMA((3 * last + 1,)),
        ],
        compiler_params=params(56),
        cost_estimate=cost(2 * D * G * TOK, 12 << 20),
        name="inner",
    )(place, *weights[N_EARLY:], early_b, normal_b, acts, weight_b, scales)
    dgs_all, _ = gather_ring(dgs)
    keep, send = pl.pallas_call(
        outer_kernel,
        in_specs=[SM] + [HB] * N_DP + [VM, VM, HB, VM, VM, VM],
        out_specs=[VM, VM],
        out_shape=[jax.ShapeDtypeStruct((N_T // 2, 2 * F + 2 * N_T, TOK), bf)] * 2,
        scratch_shapes=[
            pltpu.VMEM((N_DP, 3 * G, DS), bf),
            pltpu.VMEM((last, DS, TOK), bf),
            pltpu.VMEM((G, TOK), bf),
            pltpu.VMEM((TOK, 2 * G), bf),
            pltpu.VMEM((TOK, G), bf),
            pltpu.SemaphoreType.DMA((N_DP + last,)),
        ],
        compiler_params=params(56),
        cost_estimate=cost(8 * D * G * TOK, 28 << 20),
        name="outer",
    )(place, *weights, dg, early_f, normal_f, weight_f, scales, stat)
    send = after(send, tuple(dgs_all[1:4]))
    got = shift(send, c=1)
    got, keep = lax.optimization_barrier((got, after(keep, tuple(dgs_all[4:7]))))
    both = (keep.astype(f32) + got.astype(f32)).astype(bf)
    summed = lax.psum_scatter(both, "y", scatter_dimension=0)

    half = N_DP // 2
    sums_shape = [jax.ShapeDtypeStruct((2 * G, DS), f32)] * 2
    fetched = [
        pltpu.VMEM((half, 2, F, TOK), bf),
        pltpu.VMEM((half, 2, F, TOK), bf),
        pltpu.VMEM((half, 2 * G, TOK), bf),
    ]
    near_sum, far_sum = pl.pallas_call(
        functools.partial(grad_kernel, range(half)),
        in_specs=[SM] + [HB] * (half + 1),
        out_specs=[VM, VM],
        out_shape=sums_shape,
        scratch_shapes=fetched + [pltpu.SemaphoreType.DMA((3 * half,))],
        compiler_params=params(56),
        cost_estimate=cost(4 * DS * G * TOK * N_DP, 14 << 20),
        name="grad_first",
    )(place, *dgs_all[:half], tokens)
    near_grad, far_grad = pl.pallas_call(
        functools.partial(grad_kernel, range(half, N_DP)),
        in_specs=[SM] + [HB] * (half + 1) + [VM, HB, HB],
        out_specs=[VM, VM],
        out_shape=[jax.ShapeDtypeStruct((2 * G, DS), bf)] * 2,
        scratch_shapes=fetched
        + [pltpu.VMEM((2, 2 * G, DS), f32), pltpu.SemaphoreType.DMA((3 * half + 2,))],
        compiler_params=params(56),
        cost_estimate=cost(4 * DS * G * TOK * N_DP, 14 << 20),
        name="grad_last",
    )(place, *dgs_all[half:], tokens, gain[None, :], near_sum, far_sum)
    z = shift(near_grad, zl=1)
    behind = shift(near_grad, x=1)
    ahead = shift(near_grad, x=-1)
    z_far = shift(far_grad, zl=1)
    z_behind = shift(z, x=1)
    z_ahead = shift(z, x=-1)
    parts = [near_grad, z, behind, ahead, z_behind, z_ahead, far_grad, z_far]
    grad_g, grad_u = pl.pallas_call(
        assemble_kernel,
        in_specs=[SM] + [VM] * N_DP,
        out_specs=[VM, VM],
        out_shape=[jax.ShapeDtypeStruct((G, D), bf)] * 2,
        compiler_params=params(24),
        cost_estimate=cost(0, 8 << 20),
        name="assemble",
    )(place, *parts)

    into = summed[:F].astype(f32)
    mean_stat = jnp.sum(summed[2 * F :].astype(f32), axis=0, keepdims=True) / D
    gain_here = lax.dynamic_slice_in_dim(gain, here * F, F)[:, None]
    output = (acts_t.astype(f32) + summed[F : 2 * F].astype(f32)).astype(bf)
    scale_b = scales[0:1]
    hat = saved_t.astype(f32) * scale_b
    stored = (dy_t.astype(f32) + scale_b * (into * gain_here - hat * mean_stat)).astype(bf)
    return (output.T[None], stored.T[None], grad_g.T[None], grad_u.T[None])


def solution(mesh):
    fine = Mesh(mesh.devices.reshape(tuple(SIZES[a] for a in AXES)), AXES)
    dp, tensor = ("x", "zl"), ("y", "c")
    placed = (
        P("s", dp, tensor),
        P("s", dp, tensor),
        P("s", dp, tensor),
        P("s", None),
        P("s", dp, tensor),
        P("s", dp, tensor),
        P("s", tensor, dp),
        P("s", None, dp, None),
        P("s", None, dp, None),
    )
    return jax.shard_map(
        local,
        mesh=fine,
        in_specs=placed,
        out_specs=(
            P("s", dp, tensor),
            P("s", dp, tensor),
            P("s", None, tensor),
            P("s", None, tensor),
        ),
        check_vma=False,
    )
```

```python
import jax
import jax.numpy as jnp
import numpy as np
from jax import lax
from jax.experimental import pallas as pl
from jax.experimental.pallas import tpu as pltpu
from jax.sharding import Mesh, PartitionSpec as P

EPS = 1e-05
AXES = ("x", "zl", "s", "y", "c")
SIZES = {"x": 4, "zl": 2, "s": 4, "y": 8, "c": 2}
D = 3072
TOK = 256
G = 336
F = 192
N_T = 16
N_DP = 8
DS = D // N_DP
N_EARLY = 6
TILE = 336
OFFSETS = ((0, 0), (0, 1), (-1, 0), (1, 0), (-1, 1), (1, 1), (2, 0), (2, 1))

VM = pl.BlockSpec(memory_space=pltpu.VMEM)
HB = pl.BlockSpec(memory_space=pltpu.HBM)
SM = pl.BlockSpec(memory_space=pltpu.SMEM)


def shift(value, **steps):
    axes = tuple(a for a in AXES if a in steps)
    sizes = [SIZES[a] for a in axes]
    pairs = []
    for i in range(int(np.prod(sizes))):
        at = np.unravel_index(i, sizes)
        to = [(at[k] + steps[a]) % sizes[k] for k, a in enumerate(axes)]
        pairs.append((i, int(np.ravel_multi_index(to, sizes))))
    return lax.ppermute(value, axes if len(axes) > 1 else axes[0], pairs)


def swapped(value, step):
    pairs = []
    for e in range(N_DP):
        for y in range(N_DP):
            d = (((y // 2) + step) % 4) * 2 + y % 2
            pairs.append((e * N_DP + y, d * N_DP + e))
    return lax.ppermute(value, ("x", "zl", "y"), pairs)


def gather_ring(own, ready):
    z, behind, ahead = lax.optimization_barrier((shift(own, zl=1), shift(own, x=1), shift(own, x=-1)))
    z_behind = shift(z, x=1)
    z_ahead = shift(z, x=-1)
    across = shift(behind, x=1)
    z_ahead, ready = lax.optimization_barrier((z_ahead, ready))
    z_across = shift(z_ahead, x=-1)
    return [own, z, behind, ahead, z_behind, z_ahead, across, z_across], ready


def gather_weights(own, block, ready):
    z = shift(own, zl=1)
    behind = shift(own, x=1)
    ahead = shift(own, x=-1)
    near = swapped(block, 0)
    z, behind, ahead, near, block, ready = lax.optimization_barrier((z, behind, ahead, near, block, ready))
    z_behind = shift(z, x=1)
    z_ahead = shift(z, x=-1)
    far = swapped(block, 2)
    z_behind, z_ahead, far = lax.optimization_barrier((z_behind, z_ahead, far))
    across = shift(behind, x=1)
    z_across = shift(z_ahead, x=-1)
    return [own, z, behind, ahead, z_behind, z_ahead, across, z_across], (near, far), ready


def after(value, earlier):
    return lax.optimization_barrier((value, earlier))[0]


def places():
    x, zl = lax.axis_index("x"), lax.axis_index("zl")
    return jnp.stack([((x + dx) % 4) * 2 + (zl + dz) % 2 for dx, dz in OFFSETS]).astype(jnp.int32)


def gained_into(act_ref, gain_ref, out_ref):
    total = jnp.zeros((8, TOK), jnp.float32)
    for t in range(N_T):
        v = act_ref[t].astype(jnp.float32)
        total = total + jnp.sum((v * v).reshape(F // 8, 8, TOK), axis=0)
        out_ref[t * F : (t + 1) * F, :] = (v * gain_ref[t * F : (t + 1) * F, :]).astype(jnp.bfloat16)
    return lax.rsqrt(jnp.sum(total, axis=0, keepdims=True) / D + EPS)


def fetch(pairs, sems):
    copies = [pltpu.make_async_copy(src, dst, sems.at[i]) for i, (src, dst) in enumerate(pairs)]
    for copy in copies:
        copy.start()
    return copies


def early_kernel(place, *refs):
    w = refs[:N_EARLY]
    acts, gain, b_out, f_out, nb_out, nf_out, dy_out, scales_out, saved, dy, act, normal_b, normal_f, sems = refs[N_EARLY:]
    copies = fetch([(acts.at[:, 2], saved), (acts.at[:, 0], act), (acts.at[:, 1], dy)], sems)
    copies[0].wait()
    scales_out[0:1, :] = gained_into(saved, gain, normal_b)
    copies[1].wait()
    scales_out[1:2, :] = gained_into(act, gain, normal_f)
    copies[2].wait()
    for i in range(N_DP - N_EARLY):
        d = place[N_EARLY + i]
        rows = pl.ds(pl.multiple_of(d * DS, DS), DS)
        nb_out[i] = normal_b[rows, :]
        nf_out[i] = normal_f[rows, :]
        dy_out[i] = dy[pl.ds(2 * d, 2)].reshape(DS, TOK)
    for m in range(0, G, TILE):
        sums = [jnp.zeros((TILE, TOK), jnp.float32) for _ in range(5)]
        for r in range(N_EARLY):
            d = place[r]
            rows = pl.ds(pl.multiple_of(d * DS, DS), DS)
            n, f = normal_b[rows, :], normal_f[rows, :]
            g = dy[pl.ds(2 * d, 2)].reshape(DS, TOK)
            w_g = w[r][m : m + TILE, :]
            w_u = w[r][G + m : G + m + TILE, :]
            w_d = w[r][2 * G + m : 2 * G + m + TILE, :]
            for k, (left, right) in enumerate(((w_g, n), (w_u, n), (w_d, g), (w_g, f), (w_u, f))):
                sums[k] = sums[k] + jnp.dot(left, right, preferred_element_type=jnp.float32)
        for k in range(3):
            b_out[k * G + m : k * G + m + TILE, :] = sums[k]
        for k in range(2):
            f_out[k * G + m : k * G + m + TILE, :] = sums[3 + k]


def inner_kernel(w_6, w_7, early, normal, dy, weight, scales, dg_out, dgs_out, stat_out):
    w = (w_6, w_7)
    last = N_DP - N_EARLY
    scale = scales[0:1, :]
    row = weight[...]
    stat = jnp.zeros((1, TOK), jnp.float32)
    for m in range(0, G, TILE):
        gate, up, hid = (early[k * G + m : k * G + m + TILE, :] for k in range(3))
        for i in range(last):
            n, g = normal[i], dy[i]
            gate = gate + jnp.dot(w[i][m : m + TILE, :], n, preferred_element_type=jnp.float32)
            up = up + jnp.dot(w[i][G + m : G + m + TILE, :], n, preferred_element_type=jnp.float32)
            hid = hid + jnp.dot(w[i][2 * G + m : 2 * G + m + TILE, :], g, preferred_element_type=jnp.float32)
        gate = scale * gate
        up = scale * up
        sg = jax.nn.sigmoid(gate)
        hid = hid * row
        dgate = hid * up * (sg * (1.0 + gate * (1.0 - sg)))
        dup = hid * (gate * sg)
        dgate_r, dup_r = dgate.astype(jnp.bfloat16), dup.astype(jnp.bfloat16)
        dg_out[m : m + TILE, :] = dgate_r
        dg_out[G + m : G + m + TILE, :] = dup_r
        dgs_out[m : m + TILE, :] = (dgate * scale).astype(jnp.bfloat16)
        dgs_out[G + m : G + m + TILE, :] = (dup * scale).astype(jnp.bfloat16)
        stat = stat + jnp.sum(
            dgate_r.astype(jnp.float32) * gate + dup_r.astype(jnp.float32) * up, axis=0, keepdims=True
        )
    stat_out[...] = stat


def outer_kernel(place, *refs):
    w = refs[:N_DP]
    dg, early, normal, weight, scales, stat, out, chunks, hidden, dg_t, hid_t, sems = refs[N_DP:]
    last = N_DP - N_EARLY
    me = place[N_DP]
    value = stat[...]
    high = value.astype(jnp.bfloat16).astype(jnp.float32)
    rows = lax.broadcasted_iota(jnp.int32, (2 * N_T, TOK), 0)
    block = jnp.where(rows == me, high, jnp.where(rows == me + N_T, value - high, 0.0)).astype(jnp.bfloat16)
    for r in range(N_DP):
        for half in range(2):
            chunks[r, half, 2 * F :, :] = block
    dg_t[...] = dg[...].T
    row = weight[...]
    scale = scales[1:2, :]
    for m in range(0, G, TILE):
        gate, up = (early[k * G + m : k * G + m + TILE, :] for k in range(2))
        for i in range(last):
            n = normal[i]
            gate = gate + jnp.dot(w[N_EARLY + i][m : m + TILE, :], n, preferred_element_type=jnp.float32)
            up = up + jnp.dot(w[N_EARLY + i][G + m : G + m + TILE, :], n, preferred_element_type=jnp.float32)
        gate = scale * gate
        up = scale * up
        hidden[m : m + TILE, :] = (gate * jax.nn.sigmoid(gate) * up * row).astype(jnp.bfloat16)
    hid_t[...] = hidden[...].T
    copies = []
    for r in range(N_DP):
        into = jnp.dot(dg_t[...], w[r][: 2 * G, :], preferred_element_type=jnp.float32)
        chunks[r, :, 0:F, :] = into.astype(jnp.bfloat16).T.reshape(2, F, TOK)
        part = jnp.dot(hid_t[...], w[r][2 * G :, :], preferred_element_type=jnp.float32)
        chunks[r, :, F : 2 * F, :] = part.astype(jnp.bfloat16).T.reshape(2, F, TOK)
        copies.append(pltpu.make_async_copy(chunks.at[r], out.at[pl.ds(2 * place[r], 2)], sems.at[r]))
        copies[r].start()
    for copy in copies:
        copy.wait()


def grad_kernel(place, *refs):
    dgs = refs[:N_DP]
    tokens, gain, near_out, far_out = refs[N_DP:]
    own = place[0]
    for j, (at, out) in enumerate(((own, near_out), (lax.rem(own + 4, N_DP), far_out))):
        lanes = gain[:, pl.ds(pl.multiple_of(at * DS, DS), DS)]
        for m in range(0, 2 * G, G):
            total = jnp.zeros((G, DS), jnp.float32)
            for r in range(N_DP):
                v = tokens[pl.ds(2 * place[r], 2), j].reshape(DS, TOK)
                total = total + lax.dot_general(
                    dgs[r][m : m + G, :], v, (((1,), (1,)), ((), ())), preferred_element_type=jnp.float32
                )
            out[m : m + G, :] = (total * lanes).astype(jnp.bfloat16)


def assemble_kernel(place, *refs):
    parts = refs[:N_DP]
    gate_out, up_out, sems = refs[N_DP:]
    pairs = []
    for r in range(N_DP):
        lanes = pl.ds(pl.multiple_of(place[r] * DS, DS), DS)
        pairs += [(parts[r].at[:G, :], gate_out.at[:, lanes]), (parts[r].at[G:, :], up_out.at[:, lanes])]
    for copy in fetch(pairs, sems):
        copy.wait()


def params(mib):
    return pltpu.CompilerParams(vmem_limit_bytes=mib << 20)


def cost(flops, nbytes):
    return pl.CostEstimate(flops=flops, bytes_accessed=nbytes, transcendentals=0)


def combine(route_ids, probs):
    return jnp.sum(jnp.where(route_ids == 0, probs, jnp.zeros_like(probs)), axis=-1)[None, :]


def local(
    passed_activations,
    kept_section_input,
    handed_grads,
    norm_gain,
    gate_weight,
    up_weight,
    down_weight,
    routes,
    route_probs,
):
    place = places()
    here = lax.axis_index("y") * 2 + lax.axis_index("c")
    place_t = jnp.concatenate([place, here[None].astype(jnp.int32)])
    saved_t = kept_section_input[0].T
    acts_t = shift(passed_activations[0].T, s=1)
    dy_t = shift(handed_grads[0].T, s=-1)
    gain = norm_gain[0]
    own_weights = jnp.concatenate([gate_weight[0].T, up_weight[0].T, down_weight[0]], axis=0)
    ready = (gain[:, None], place_t, combine(routes[0, 0], route_probs[0, 0]), combine(routes[0, 1], route_probs[0, 1]))
    weights, swaps, ready = gather_weights(own_weights, saved_t, ready)
    gain_col, place, weight_f, weight_b = ready
    acts = lax.all_gather(
        after(jnp.concatenate([acts_t, dy_t, saved_t], axis=0), own_weights), ("y", "c"), axis=0
    ).reshape(N_T, 3, F, TOK)
    tokens = lax.all_gather(jnp.concatenate(swaps, axis=0), ("y", "c"), axis=0).reshape(N_T, 2, F, TOK)

    bf, f32 = jnp.bfloat16, jnp.float32
    last = N_DP - N_EARLY
    block = jax.ShapeDtypeStruct((last, DS, TOK), bf)
    early_b, early_f, normal_b, normal_f, dy_last, scales = pl.pallas_call(
        early_kernel,
        in_specs=[SM] + [VM] * N_EARLY + [HB, VM],
        out_specs=[VM] * 6,
        out_shape=[
            jax.ShapeDtypeStruct((3 * G, TOK), f32),
            jax.ShapeDtypeStruct((2 * G, TOK), f32),
            block,
            block,
            block,
            jax.ShapeDtypeStruct((2, TOK), f32),
        ],
        scratch_shapes=[
            pltpu.VMEM((N_T, F, TOK), bf),
            pltpu.VMEM((N_T, F, TOK), bf),
            pltpu.VMEM((N_T, F, TOK), bf),
            pltpu.VMEM((D, TOK), bf),
            pltpu.VMEM((D, TOK), bf),
            pltpu.SemaphoreType.DMA((3,)),
        ],
        compiler_params=params(20),
        cost_estimate=cost(10 * D * G * TOK, 28 << 20),
        name="early",
    )(place, *weights[:N_EARLY], acts, gain_col)
    dg, dgs, stat = pl.pallas_call(
        inner_kernel,
        in_specs=[VM] * 7,
        out_specs=[VM] * 3,
        out_shape=[
            jax.ShapeDtypeStruct((2 * G, TOK), bf),
            jax.ShapeDtypeStruct((2 * G, TOK), bf),
            jax.ShapeDtypeStruct((1, TOK), f32),
        ],
        compiler_params=params(12),
        cost_estimate=cost(2 * D * G * TOK, 8 << 20),
        name="inner",
    )(*weights[N_EARLY:], early_b, normal_b, dy_last, weight_b, scales)
    dgs_all, tokens = gather_ring(dgs, tokens)
    payload = pl.pallas_call(
        outer_kernel,
        in_specs=[SM] + [VM] * (N_DP + 6),
        out_specs=HB,
        out_shape=jax.ShapeDtypeStruct((N_T, 2 * F + 2 * N_T, TOK), bf),
        scratch_shapes=[
            pltpu.VMEM((N_DP, 2, 2 * F + 2 * N_T, TOK), bf),
            pltpu.VMEM((G, TOK), bf),
            pltpu.VMEM((TOK, 2 * G), bf),
            pltpu.VMEM((TOK, G), bf),
            pltpu.SemaphoreType.DMA((N_DP,)),
        ],
        compiler_params=params(16),
        cost_estimate=cost(8 * D * G * TOK, 20 << 20),
        name="outer",
    )(place, *weights, dg, early_f, normal_f, weight_f, scales, stat)
    summed = lax.psum_scatter(payload, ("y", "c"), scatter_dimension=0)

    near_grad, far_grad = pl.pallas_call(
        grad_kernel,
        in_specs=[SM] + [VM] * (N_DP + 2),
        out_specs=[VM, VM],
        out_shape=[jax.ShapeDtypeStruct((2 * G, DS), bf)] * 2,
        compiler_params=params(12),
        cost_estimate=cost(8 * DS * G * TOK * N_DP, 8 << 20),
        name="grad",
    )(place, *dgs_all, tokens, gain[None, :])
    z = shift(near_grad, zl=1)
    behind = shift(near_grad, x=1)
    ahead = shift(near_grad, x=-1)
    z_far = shift(far_grad, zl=1)
    z_behind = shift(z, x=1)
    z_ahead = shift(z, x=-1)
    parts = [near_grad, z, behind, ahead, z_behind, z_ahead, far_grad, z_far]
    grad_g, grad_u = pl.pallas_call(
        assemble_kernel,
        in_specs=[SM] + [VM] * N_DP,
        out_specs=[HB, HB],
        out_shape=[jax.ShapeDtypeStruct((G, D), bf)] * 2,
        scratch_shapes=[pltpu.SemaphoreType.DMA((2 * N_DP,))],
        compiler_params=params(12),
        cost_estimate=cost(0, 8 << 20),
        name="assemble",
    )(place, *parts)

    into = summed[:F].astype(f32)
    mean_stat = jnp.sum(summed[2 * F :].astype(f32), axis=0, keepdims=True) / D
    gain_here = lax.dynamic_slice_in_dim(gain, here * F, F)[:, None]
    output = (acts_t.astype(f32) + summed[F : 2 * F].astype(f32)).astype(bf)
    scale_b = scales[0:1]
    hat = saved_t.astype(f32) * scale_b
    stored = (dy_t.astype(f32) + scale_b * (into * gain_here - hat * mean_stat)).astype(bf)
    return (output.T[None], stored.T[None], grad_g.T[None], grad_u.T[None])


def solution(mesh):
    fine = Mesh(mesh.devices.reshape(tuple(SIZES[a] for a in AXES)), AXES)
    dp, tensor = ("x", "zl"), ("y", "c")
    placed = (
        P("s", dp, tensor),
        P("s", dp, tensor),
        P("s", dp, tensor),
        P("s", None),
        P("s", dp, tensor),
        P("s", dp, tensor),
        P("s", tensor, dp),
        P("s", None, dp, None),
        P("s", None, dp, None),
    )
    return jax.shard_map(
        local,
        mesh=fine,
        in_specs=placed,
        out_specs=(
            P("s", dp, tensor),
            P("s", dp, tensor),
            P("s", None, tensor),
            P("s", None, tensor),
        ),
        check_vma=False,
    )
```

```python
import jax
import jax.numpy as jnp
import numpy as np
from jax import lax
from jax.experimental import pallas as pl
from jax.experimental.pallas import tpu as pltpu
from jax.sharding import Mesh, PartitionSpec as P

EPS = 1e-05
AXES = ("x", "zl", "s", "y", "c")
SIZES = {"x": 4, "zl": 2, "s": 4, "y": 8, "c": 2}
D = 3072
TOK = 256
G = 336
F = 192
N_T = 16
N_DP = 8
DS = D // N_DP
N_EARLY = 6
TILE = 336
OFFSETS = ((0, 0), (0, 1), (-1, 0), (1, 0), (-1, 1), (1, 1), (2, 0), (2, 1))

VM = pl.BlockSpec(memory_space=pltpu.VMEM)
HB = pl.BlockSpec(memory_space=pltpu.HBM)
SM = pl.BlockSpec(memory_space=pltpu.SMEM)


def shift(value, **steps):
    axes = tuple(a for a in AXES if a in steps)
    sizes = [SIZES[a] for a in axes]
    pairs = []
    for i in range(int(np.prod(sizes))):
        at = np.unravel_index(i, sizes)
        to = [(at[k] + steps[a]) % sizes[k] for k, a in enumerate(axes)]
        pairs.append((i, int(np.ravel_multi_index(to, sizes))))
    return lax.ppermute(value, axes if len(axes) > 1 else axes[0], pairs)


def swapped(value, step):
    pairs = []
    for e in range(N_DP):
        for y in range(N_DP):
            d = (((y // 2) + step) % 4) * 2 + y % 2
            pairs.append((e * N_DP + y, d * N_DP + e))
    return lax.ppermute(value, ("x", "zl", "y"), pairs)


def gather_ring(own, ready):
    z, behind, ahead = lax.optimization_barrier((shift(own, zl=1), shift(own, x=1), shift(own, x=-1)))
    z_behind = shift(z, x=1)
    z_ahead = shift(z, x=-1)
    across = shift(behind, x=1)
    z_ahead, ready = lax.optimization_barrier((z_ahead, ready))
    z_across = shift(z_ahead, x=-1)
    return [own, z, behind, ahead, z_behind, z_ahead, across, z_across], ready


def gather_weights(own, block, ready):
    z = shift(own, zl=1)
    behind = shift(own, x=1)
    ahead = shift(own, x=-1)
    near = swapped(block, 0)
    z, behind, ahead, near, block, ready = lax.optimization_barrier((z, behind, ahead, near, block, ready))
    z_behind = shift(z, x=1)
    z_ahead = shift(z, x=-1)
    far = swapped(block, 2)
    z_behind, z_ahead, far = lax.optimization_barrier((z_behind, z_ahead, far))
    across = shift(behind, x=1)
    z_across = shift(z_ahead, x=-1)
    return [own, z, behind, ahead, z_behind, z_ahead, across, z_across], (near, far), ready


def after(value, earlier):
    return lax.optimization_barrier((value, earlier))[0]


def places():
    x, zl = lax.axis_index("x"), lax.axis_index("zl")
    return jnp.stack([((x + dx) % 4) * 2 + (zl + dz) % 2 for dx, dz in OFFSETS]).astype(jnp.int32)


def gained_into(act_ref, gain_ref, out_ref):
    total = jnp.zeros((8, TOK), jnp.float32)
    for t in range(N_T):
        v = act_ref[t].astype(jnp.float32)
        total = total + jnp.sum((v * v).reshape(F // 8, 8, TOK), axis=0)
        out_ref[t * F : (t + 1) * F, :] = (v * gain_ref[t * F : (t + 1) * F, :]).astype(jnp.bfloat16)
    return lax.rsqrt(jnp.sum(total, axis=0, keepdims=True) / D + EPS)


def fetch(pairs, sems):
    copies = [pltpu.make_async_copy(src, dst, sems.at[i]) for i, (src, dst) in enumerate(pairs)]
    for copy in copies:
        copy.start()
    return copies


def early_kernel(place, *refs):
    w = refs[:N_EARLY]
    acts, gain, b_out, f_out, nb_out, nf_out, dy_out, scales_out, saved, dy, act, normal_b, normal_f, sems = refs[N_EARLY:]
    copies = fetch([(acts.at[:, 2], saved), (acts.at[:, 0], act), (acts.at[:, 1], dy)], sems)
    copies[0].wait()
    scales_out[0:1, :] = gained_into(saved, gain, normal_b)
    copies[1].wait()
    scales_out[1:2, :] = gained_into(act, gain, normal_f)
    copies[2].wait()
    for i in range(N_DP - N_EARLY):
        d = place[N_EARLY + i]
        rows = pl.ds(pl.multiple_of(d * DS, DS), DS)
        nb_out[i] = normal_b[rows, :]
        nf_out[i] = normal_f[rows, :]
        dy_out[i] = dy[pl.ds(2 * d, 2)].reshape(DS, TOK)
    for m in range(0, G, TILE):
        sums = [jnp.zeros((TILE, TOK), jnp.float32) for _ in range(5)]
        for r in range(N_EARLY):
            d = place[r]
            rows = pl.ds(pl.multiple_of(d * DS, DS), DS)
            n, f = normal_b[rows, :], normal_f[rows, :]
            g = dy[pl.ds(2 * d, 2)].reshape(DS, TOK)
            w_g = w[r][m : m + TILE, :]
            w_u = w[r][G + m : G + m + TILE, :]
            w_d = w[r][2 * G + m : 2 * G + m + TILE, :]
            for k, (left, right) in enumerate(((w_g, n), (w_u, n), (w_d, g), (w_g, f), (w_u, f))):
                sums[k] = sums[k] + jnp.dot(left, right, preferred_element_type=jnp.float32)
        for k in range(3):
            b_out[k * G + m : k * G + m + TILE, :] = sums[k]
        for k in range(2):
            f_out[k * G + m : k * G + m + TILE, :] = sums[3 + k]


def inner_kernel(w_6, w_7, early, normal, dy, weight, scales, dg_out, dgs_out, stat_out):
    w = (w_6, w_7)
    last = N_DP - N_EARLY
    scale = scales[0:1, :]
    row = weight[...]
    stat = jnp.zeros((1, TOK), jnp.float32)
    for m in range(0, G, TILE):
        gate, up, hid = (early[k * G + m : k * G + m + TILE, :] for k in range(3))
        for i in range(last):
            n, g = normal[i], dy[i]
            gate = gate + jnp.dot(w[i][m : m + TILE, :], n, preferred_element_type=jnp.float32)
            up = up + jnp.dot(w[i][G + m : G + m + TILE, :], n, preferred_element_type=jnp.float32)
            hid = hid + jnp.dot(w[i][2 * G + m : 2 * G + m + TILE, :], g, preferred_element_type=jnp.float32)
        gate = scale * gate
        up = scale * up
        sg = jax.nn.sigmoid(gate)
        hid = hid * row
        dgate = hid * up * (sg * (1.0 + gate * (1.0 - sg)))
        dup = hid * (gate * sg)
        dgate_r, dup_r = dgate.astype(jnp.bfloat16), dup.astype(jnp.bfloat16)
        dg_out[m : m + TILE, :] = dgate_r
        dg_out[G + m : G + m + TILE, :] = dup_r
        dgs_out[m : m + TILE, :] = (dgate * scale).astype(jnp.bfloat16)
        dgs_out[G + m : G + m + TILE, :] = (dup * scale).astype(jnp.bfloat16)
        stat = stat + jnp.sum(
            dgate_r.astype(jnp.float32) * gate + dup_r.astype(jnp.float32) * up, axis=0, keepdims=True
        )
    stat_out[...] = stat


def outer_kernel(place, *refs):
    w = refs[:N_DP]
    dg, early, normal, weight, scales, stat, out, chunks, hidden, dg_t, hid_t, sems = refs[N_DP:]
    last = N_DP - N_EARLY
    me = place[N_DP]
    value = stat[...]
    high = value.astype(jnp.bfloat16).astype(jnp.float32)
    rows = lax.broadcasted_iota(jnp.int32, (2 * N_T, TOK), 0)
    block = jnp.where(rows == me, high, jnp.where(rows == me + N_T, value - high, 0.0)).astype(jnp.bfloat16)
    first = lax.rem(me, 2) == 0
    for r in range(N_DP):
        for half in range(2):
            chunks[r, half, 2 * F :, :] = block
    dg_t[...] = dg[...].T
    row = weight[...]
    scale = scales[1:2, :]
    for m in range(0, G, TILE):
        gate, up = (early[k * G + m : k * G + m + TILE, :] for k in range(2))
        for i in range(last):
            n = normal[i]
            gate = gate + jnp.dot(w[N_EARLY + i][m : m + TILE, :], n, preferred_element_type=jnp.float32)
            up = up + jnp.dot(w[N_EARLY + i][G + m : G + m + TILE, :], n, preferred_element_type=jnp.float32)
        gate = scale * gate
        up = scale * up
        hidden[m : m + TILE, :] = (gate * jax.nn.sigmoid(gate) * up * row).astype(jnp.bfloat16)
    hid_t[...] = hidden[...].T
    copies = []
    for r in range(N_DP):
        into = jnp.dot(dg_t[...], w[r][: 2 * G, :], preferred_element_type=jnp.float32)
        part = jnp.dot(hid_t[...], w[r][2 * G :, :], preferred_element_type=jnp.float32)
        for value, low in ((into, 0), (part, F)):
            value = value.astype(jnp.bfloat16).T
            one, two = value[:F], value[F:]
            chunks[r, 0, low : low + F, :] = jnp.where(first, one, two)
            chunks[r, 1, low : low + F, :] = jnp.where(first, two, one)
        copies.append(pltpu.make_async_copy(chunks.at[r], out.at[place[r]], sems.at[r]))
        copies[r].start()
    for copy in copies:
        copy.wait()


def grad_kernel(place, *refs):
    dgs = refs[:N_DP]
    tokens, gain, near_out, far_out = refs[N_DP:]
    own = place[0]
    for j, (at, out) in enumerate(((own, near_out), (lax.rem(own + 4, N_DP), far_out))):
        lanes = gain[:, pl.ds(pl.multiple_of(at * DS, DS), DS)]
        for m in range(0, 2 * G, G):
            total = jnp.zeros((G, DS), jnp.float32)
            for r in range(N_DP):
                v = tokens[pl.ds(2 * place[r], 2), j].reshape(DS, TOK)
                total = total + lax.dot_general(
                    dgs[r][m : m + G, :], v, (((1,), (1,)), ((), ())), preferred_element_type=jnp.float32
                )
            out[m : m + G, :] = (total * lanes).astype(jnp.bfloat16)


def assemble_kernel(place, *refs):
    parts = refs[:N_DP]
    gate_out, up_out, sems = refs[N_DP:]
    pairs = []
    for r in range(N_DP):
        lanes = pl.ds(pl.multiple_of(place[r] * DS, DS), DS)
        pairs += [(parts[r].at[:G, :], gate_out.at[:, lanes]), (parts[r].at[G:, :], up_out.at[:, lanes])]
    for copy in fetch(pairs, sems):
        copy.wait()


def finish_kernel(summed, got, act, saved, dy, scales, gain, output, stored):
    f32 = jnp.float32
    scale = scales[0:1, :]

    def rows(low, high):
        return summed[0, low:high, :].astype(f32) + got[low:high, :].astype(f32)

    mean = jnp.sum(rows(2 * F, 2 * F + 2 * N_T), axis=0, keepdims=True) / D
    output[...] = (act[...].astype(f32) + rows(F, 2 * F)).astype(jnp.bfloat16)
    hat = saved[...].astype(f32) * scale
    stored[...] = (dy[...].astype(f32) + scale * (rows(0, F) * gain[...] - hat * mean)).astype(jnp.bfloat16)


def params(mib):
    return pltpu.CompilerParams(vmem_limit_bytes=mib << 20)


def cost(flops, nbytes):
    return pl.CostEstimate(flops=flops, bytes_accessed=nbytes, transcendentals=0)


def combine(route_ids, probs):
    return jnp.sum(jnp.where(route_ids == 0, probs, jnp.zeros_like(probs)), axis=-1)[None, :]


def local(
    passed_activations,
    kept_section_input,
    handed_grads,
    norm_gain,
    gate_weight,
    up_weight,
    down_weight,
    routes,
    route_probs,
):
    place = places()
    here = lax.axis_index("y") * 2 + lax.axis_index("c")
    place_t = jnp.concatenate([place, here[None].astype(jnp.int32)])
    saved_t = kept_section_input[0].T
    acts_t = shift(passed_activations[0].T, s=1)
    dy_t = shift(handed_grads[0].T, s=-1)
    gain = norm_gain[0]
    own_weights = jnp.concatenate([gate_weight[0].T, up_weight[0].T, down_weight[0]], axis=0)
    ready = (gain[:, None], place_t, combine(routes[0, 0], route_probs[0, 0]), combine(routes[0, 1], route_probs[0, 1]))
    weights, swaps, ready = gather_weights(own_weights, saved_t, ready)
    gain_col, place, weight_f, weight_b = ready
    acts = lax.all_gather(
        after(jnp.concatenate([acts_t, dy_t, saved_t], axis=0), own_weights), ("y", "c"), axis=0
    ).reshape(N_T, 3, F, TOK)
    tokens = lax.all_gather(jnp.concatenate(swaps, axis=0), ("y", "c"), axis=0).reshape(N_T, 2, F, TOK)

    bf, f32 = jnp.bfloat16, jnp.float32
    last = N_DP - N_EARLY
    block = jax.ShapeDtypeStruct((last, DS, TOK), bf)
    early_b, early_f, normal_b, normal_f, dy_last, scales = pl.pallas_call(
        early_kernel,
        in_specs=[SM] + [VM] * N_EARLY + [HB, VM],
        out_specs=[VM] * 6,
        out_shape=[
            jax.ShapeDtypeStruct((3 * G, TOK), f32),
            jax.ShapeDtypeStruct((2 * G, TOK), f32),
            block,
            block,
            block,
            jax.ShapeDtypeStruct((2, TOK), f32),
        ],
        scratch_shapes=[
            pltpu.VMEM((N_T, F, TOK), bf),
            pltpu.VMEM((N_T, F, TOK), bf),
            pltpu.VMEM((N_T, F, TOK), bf),
            pltpu.VMEM((D, TOK), bf),
            pltpu.VMEM((D, TOK), bf),
            pltpu.SemaphoreType.DMA((3,)),
        ],
        compiler_params=params(20),
        cost_estimate=cost(10 * D * G * TOK, 28 << 20),
        name="early",
    )(place, *weights[:N_EARLY], acts, gain_col)
    dg, dgs, stat = pl.pallas_call(
        inner_kernel,
        in_specs=[VM] * 7,
        out_specs=[VM] * 3,
        out_shape=[
            jax.ShapeDtypeStruct((2 * G, TOK), bf),
            jax.ShapeDtypeStruct((2 * G, TOK), bf),
            jax.ShapeDtypeStruct((1, TOK), f32),
        ],
        compiler_params=params(12),
        cost_estimate=cost(2 * D * G * TOK, 8 << 20),
        name="inner",
    )(*weights[N_EARLY:], early_b, normal_b, dy_last, weight_b, scales)
    dgs_all, tokens = gather_ring(dgs, tokens)
    payload = pl.pallas_call(
        outer_kernel,
        in_specs=[SM] + [VM] * (N_DP + 6),
        out_specs=HB,
        out_shape=jax.ShapeDtypeStruct((N_T // 2, 2, 2 * F + 2 * N_T, TOK), bf),
        scratch_shapes=[
            pltpu.VMEM((N_DP, 2, 2 * F + 2 * N_T, TOK), bf),
            pltpu.VMEM((G, TOK), bf),
            pltpu.VMEM((TOK, 2 * G), bf),
            pltpu.VMEM((TOK, G), bf),
            pltpu.SemaphoreType.DMA((N_DP,)),
        ],
        compiler_params=params(16),
        cost_estimate=cost(8 * D * G * TOK, 20 << 20),
        name="outer",
    )(place, *weights, dg, early_f, normal_f, weight_f, scales, stat)
    payload = after(payload, tuple(dgs_all[1:4]))
    summed = lax.psum_scatter(payload, "y", scatter_dimension=0)

    near_grad, far_grad = pl.pallas_call(
        grad_kernel,
        in_specs=[SM] + [VM] * (N_DP + 2),
        out_specs=[VM, VM],
        out_shape=[jax.ShapeDtypeStruct((2 * G, DS), bf)] * 2,
        compiler_params=params(12),
        cost_estimate=cost(8 * DS * G * TOK * N_DP, 8 << 20),
        name="grad",
    )(place, *dgs_all, tokens, gain[None, :])
    z = shift(near_grad, zl=1)
    behind = shift(near_grad, x=1)
    ahead = shift(near_grad, x=-1)
    z_far = shift(far_grad, zl=1)
    got = shift(summed[1], c=1)
    z_behind = shift(z, x=1)
    z_ahead = shift(z, x=-1)
    parts = [near_grad, z, behind, ahead, z_behind, z_ahead, far_grad, z_far]
    *parts, got = lax.optimization_barrier((*parts, got))
    grad_g, grad_u = pl.pallas_call(
        assemble_kernel,
        in_specs=[SM] + [VM] * N_DP,
        out_specs=[HB, HB],
        out_shape=[jax.ShapeDtypeStruct((G, D), bf)] * 2,
        scratch_shapes=[pltpu.SemaphoreType.DMA((2 * N_DP,))],
        compiler_params=params(12),
        cost_estimate=cost(0, 8 << 20),
        name="assemble",
    )(place, *parts)

    gain_here = lax.dynamic_slice_in_dim(gain, here * F, F)[:, None]
    output, stored = pl.pallas_call(
        finish_kernel,
        in_specs=[VM] * 7,
        out_specs=[VM, VM],
        out_shape=[jax.ShapeDtypeStruct((F, TOK), bf)] * 2,
        compiler_params=params(8),
        cost_estimate=cost(20 * F * TOK, 2 << 20),
        name="finish",
    )(summed, got, acts_t, saved_t, dy_t, scales, gain_here)
    return (output.T[None], stored.T[None], grad_g.T[None], grad_u.T[None])


def solution(mesh):
    fine = Mesh(mesh.devices.reshape(tuple(SIZES[a] for a in AXES)), AXES)
    dp, tensor = ("x", "zl"), ("y", "c")
    placed = (
        P("s", dp, tensor),
        P("s", dp, tensor),
        P("s", dp, tensor),
        P("s", None),
        P("s", dp, tensor),
        P("s", dp, tensor),
        P("s", tensor, dp),
        P("s", None, dp, None),
        P("s", None, dp, None),
    )
    return jax.shard_map(
        local,
        mesh=fine,
        in_specs=placed,
        out_specs=(
            P("s", dp, tensor),
            P("s", dp, tensor),
            P("s", None, tensor),
            P("s", None, tensor),
        ),
        check_vma=False,
    )
```

```python
import jax
import jax.numpy as jnp
import numpy as np
from jax import lax
from jax.experimental import pallas as pl
from jax.experimental.pallas import tpu as pltpu
from jax.sharding import Mesh, PartitionSpec as P

EPS = 1e-05
AXES = ("x", "zl", "s", "y", "c")
SIZES = {"x": 4, "zl": 2, "s": 4, "y": 8, "c": 2}
D = 3072
TOK = 256
G = 336
F = 192
N_T = 16
N_DP = 8
DS = D // N_DP
N_EARLY = 6
TILE = 336
OFFSETS = ((0, 0), (0, 1), (-1, 0), (1, 0), (-1, 1), (1, 1), (2, 0), (2, 1))

VM = pl.BlockSpec(memory_space=pltpu.VMEM)
HB = pl.BlockSpec(memory_space=pltpu.HBM)
SM = pl.BlockSpec(memory_space=pltpu.SMEM)


def shift(value, **steps):
    axes = tuple(a for a in AXES if a in steps)
    sizes = [SIZES[a] for a in axes]
    pairs = []
    for i in range(int(np.prod(sizes))):
        at = np.unravel_index(i, sizes)
        to = [(at[k] + steps[a]) % sizes[k] for k, a in enumerate(axes)]
        pairs.append((i, int(np.ravel_multi_index(to, sizes))))
    return lax.ppermute(value, axes if len(axes) > 1 else axes[0], pairs)


def swapped(value, step):
    pairs = []
    for e in range(N_DP):
        for y in range(N_DP):
            d = (((y // 2) + step) % 4) * 2 + y % 2
            pairs.append((e * N_DP + y, d * N_DP + e))
    return lax.ppermute(value, ("x", "zl", "y"), pairs)


def gather_ring(own, ready):
    z, behind, ahead = lax.optimization_barrier((shift(own, zl=1), shift(own, x=1), shift(own, x=-1)))
    z_behind = shift(z, x=1)
    z_ahead = shift(z, x=-1)
    across = shift(behind, x=1)
    z_ahead, ready = lax.optimization_barrier((z_ahead, ready))
    z_across = shift(z_ahead, x=-1)
    return [own, z, behind, ahead, z_behind, z_ahead, across, z_across], ready


def gather_weights(own, block, ready):
    z = shift(own, zl=1)
    behind = shift(own, x=1)
    ahead = shift(own, x=-1)
    near = swapped(block, 0)
    z, behind, ahead, near, block, ready = lax.optimization_barrier((z, behind, ahead, near, block, ready))
    z_behind = shift(z, x=1)
    z_ahead = shift(z, x=-1)
    far = swapped(block, 2)
    z_behind, z_ahead, far = lax.optimization_barrier((z_behind, z_ahead, far))
    across = shift(behind, x=1)
    z_across = shift(z_ahead, x=-1)
    return [own, z, behind, ahead, z_behind, z_ahead, across, z_across], (near, far), ready


def after(value, earlier):
    return lax.optimization_barrier((value, earlier))[0]


def places():
    x, zl = lax.axis_index("x"), lax.axis_index("zl")
    return jnp.stack([((x + dx) % 4) * 2 + (zl + dz) % 2 for dx, dz in OFFSETS]).astype(jnp.int32)


def gained_into(act_ref, gain_ref, out_ref):
    total = jnp.zeros((8, TOK), jnp.float32)
    for t in range(N_T):
        v = act_ref[t].astype(jnp.float32)
        total = total + jnp.sum((v * v).reshape(F // 8, 8, TOK), axis=0)
        out_ref[t * F : (t + 1) * F, :] = (v * gain_ref[t * F : (t + 1) * F, :]).astype(jnp.bfloat16)
    return lax.rsqrt(jnp.sum(total, axis=0, keepdims=True) / D + EPS)


def fetch(pairs, sems):
    copies = [pltpu.make_async_copy(src, dst, sems.at[i]) for i, (src, dst) in enumerate(pairs)]
    for copy in copies:
        copy.start()
    return copies


def early_kernel(place, *refs):
    w = refs[:N_EARLY]
    acts, gain, b_out, f_out, nb_out, nf_out, dy_out, scales_out, saved, dy, act, normal_b, normal_f, sems = refs[N_EARLY:]
    copies = fetch([(acts.at[:, 2], saved), (acts.at[:, 0], act), (acts.at[:, 1], dy)], sems)
    copies[0].wait()
    scales_out[0:1, :] = gained_into(saved, gain, normal_b)
    copies[1].wait()
    scales_out[1:2, :] = gained_into(act, gain, normal_f)
    copies[2].wait()
    for i in range(N_DP - N_EARLY):
        d = place[N_EARLY + i]
        rows = pl.ds(pl.multiple_of(d * DS, DS), DS)
        nb_out[i] = normal_b[rows, :]
        nf_out[i] = normal_f[rows, :]
        dy_out[i] = dy[pl.ds(2 * d, 2)].reshape(DS, TOK)
    for m in range(0, G, TILE):
        sums = [jnp.zeros((TILE, TOK), jnp.float32) for _ in range(5)]
        for r in range(N_EARLY):
            d = place[r]
            rows = pl.ds(pl.multiple_of(d * DS, DS), DS)
            n, f = normal_b[rows, :], normal_f[rows, :]
            g = dy[pl.ds(2 * d, 2)].reshape(DS, TOK)
            w_g = w[r][m : m + TILE, :]
            w_u = w[r][G + m : G + m + TILE, :]
            w_d = w[r][2 * G + m : 2 * G + m + TILE, :]
            for k, (left, right) in enumerate(((w_g, n), (w_u, n), (w_d, g), (w_g, f), (w_u, f))):
                sums[k] = sums[k] + jnp.dot(left, right, preferred_element_type=jnp.float32)
        for k in range(3):
            b_out[k * G + m : k * G + m + TILE, :] = sums[k]
        for k in range(2):
            f_out[k * G + m : k * G + m + TILE, :] = sums[3 + k]


def inner_kernel(w_6, w_7, early, normal, dy, weight, scales, dg_out, dgs_out, stat_out):
    w = (w_6, w_7)
    last = N_DP - N_EARLY
    scale = scales[0:1, :]
    row = weight[...]
    stat = jnp.zeros((1, TOK), jnp.float32)
    for m in range(0, G, TILE):
        gate, up, hid = (early[k * G + m : k * G + m + TILE, :] for k in range(3))
        for i in range(last):
            n, g = normal[i], dy[i]
            gate = gate + jnp.dot(w[i][m : m + TILE, :], n, preferred_element_type=jnp.float32)
            up = up + jnp.dot(w[i][G + m : G + m + TILE, :], n, preferred_element_type=jnp.float32)
            hid = hid + jnp.dot(w[i][2 * G + m : 2 * G + m + TILE, :], g, preferred_element_type=jnp.float32)
        gate = scale * gate
        up = scale * up
        sg = jax.nn.sigmoid(gate)
        hid = hid * row
        dgate = hid * up * (sg * (1.0 + gate * (1.0 - sg)))
        dup = hid * (gate * sg)
        dgate_r, dup_r = dgate.astype(jnp.bfloat16), dup.astype(jnp.bfloat16)
        dg_out[m : m + TILE, :] = dgate_r
        dg_out[G + m : G + m + TILE, :] = dup_r
        dgs_out[m : m + TILE, :] = (dgate * scale).astype(jnp.bfloat16)
        dgs_out[G + m : G + m + TILE, :] = (dup * scale).astype(jnp.bfloat16)
        stat = stat + jnp.sum(
            dgate_r.astype(jnp.float32) * gate + dup_r.astype(jnp.float32) * up, axis=0, keepdims=True
        )
    stat_out[...] = stat


def outer_kernel(place, *refs):
    w = refs[:N_DP]
    dg, early, normal, weight, scales, stat, out, chunks, hidden, dg_t, hid_t, sems = refs[N_DP:]
    last = N_DP - N_EARLY
    me = place[N_DP]
    value = stat[...]
    high = value.astype(jnp.bfloat16).astype(jnp.float32)
    rows = lax.broadcasted_iota(jnp.int32, (2 * N_T, TOK), 0)
    block = jnp.where(rows == me, high, jnp.where(rows == me + N_T, value - high, 0.0)).astype(jnp.bfloat16)
    first = lax.rem(me, 2) == 0
    for r in range(N_DP):
        for half in range(2):
            chunks[r, half, 2 * F :, :] = block
    dg_t[...] = dg[...].T
    row = weight[...]
    scale = scales[1:2, :]
    for m in range(0, G, TILE):
        gate, up = (early[k * G + m : k * G + m + TILE, :] for k in range(2))
        for i in range(last):
            n = normal[i]
            gate = gate + jnp.dot(w[N_EARLY + i][m : m + TILE, :], n, preferred_element_type=jnp.float32)
            up = up + jnp.dot(w[N_EARLY + i][G + m : G + m + TILE, :], n, preferred_element_type=jnp.float32)
        gate = scale * gate
        up = scale * up
        hidden[m : m + TILE, :] = (gate * jax.nn.sigmoid(gate) * up * row).astype(jnp.bfloat16)
    hid_t[...] = hidden[...].T
    copies = []
    for r in range(N_DP):
        into = jnp.dot(dg_t[...], w[r][: 2 * G, :], preferred_element_type=jnp.float32)
        part = jnp.dot(hid_t[...], w[r][2 * G :, :], preferred_element_type=jnp.float32)
        for value, low in ((into, 0), (part, F)):
            value = value.astype(jnp.bfloat16).T
            one, two = value[:F], value[F:]
            chunks[r, 0, low : low + F, :] = jnp.where(first, one, two)
            chunks[r, 1, low : low + F, :] = jnp.where(first, two, one)
        copies.append(pltpu.make_async_copy(chunks.at[r], out.at[place[r]], sems.at[r]))
        copies[r].start()
    for copy in copies:
        copy.wait()


def grad_kernel(place, *refs):
    dgs = refs[:N_DP]
    tokens, gain, near_out, far_out = refs[N_DP:]
    own = place[0]
    for j, (at, out) in enumerate(((own, near_out), (lax.rem(own + 4, N_DP), far_out))):
        lanes = gain[:, pl.ds(pl.multiple_of(at * DS, DS), DS)]
        for m in range(0, 2 * G, G):
            total = jnp.zeros((G, DS), jnp.float32)
            for r in range(N_DP):
                v = tokens[pl.ds(2 * place[r], 2), j].reshape(DS, TOK)
                total = total + lax.dot_general(
                    dgs[r][m : m + G, :], v, (((1,), (1,)), ((), ())), preferred_element_type=jnp.float32
                )
            out[m : m + G, :] = (total * lanes).astype(jnp.bfloat16)


def assemble_kernel(place, *refs):
    parts = refs[:N_DP]
    gate_out, up_out, sems = refs[N_DP:]
    pairs = []
    for r in range(N_DP):
        lanes = pl.ds(pl.multiple_of(place[r] * DS, DS), DS)
        pairs += [(parts[r].at[:G, :], gate_out.at[:, lanes]), (parts[r].at[G:, :], up_out.at[:, lanes])]
    for copy in fetch(pairs, sems):
        copy.wait()


def finish_kernel(summed, got, act, saved, dy, scales, gain, output, stored):
    f32 = jnp.float32
    scale = scales[0:1, :]

    def rows(low, high):
        return summed[0, low:high, :].astype(f32) + got[1, low:high, :].astype(f32)

    mean = jnp.sum(rows(2 * F, 2 * F + 2 * N_T), axis=0, keepdims=True) / D
    output[...] = (act[...].astype(f32) + rows(F, 2 * F)).astype(jnp.bfloat16)
    hat = saved[...].astype(f32) * scale
    stored[...] = (dy[...].astype(f32) + scale * (rows(0, F) * gain[...] - hat * mean)).astype(jnp.bfloat16)


def params(mib):
    return pltpu.CompilerParams(vmem_limit_bytes=mib << 20)


def cost(flops, nbytes):
    return pl.CostEstimate(flops=flops, bytes_accessed=nbytes, transcendentals=0)


def combine(route_ids, probs):
    return jnp.sum(jnp.where(route_ids == 0, probs, jnp.zeros_like(probs)), axis=-1)[None, :]


def local(
    passed_activations,
    kept_section_input,
    handed_grads,
    norm_gain,
    gate_weight,
    up_weight,
    down_weight,
    routes,
    route_probs,
):
    place = places()
    here = lax.axis_index("y") * 2 + lax.axis_index("c")
    place_t = jnp.concatenate([place, here[None].astype(jnp.int32)])
    saved_t = kept_section_input[0].T
    acts_t = shift(passed_activations[0].T, s=1)
    dy_t = shift(handed_grads[0].T, s=-1)
    gain = norm_gain[0]
    own_weights = jnp.concatenate([gate_weight[0].T, up_weight[0].T, down_weight[0]], axis=0)
    ready = (gain[:, None], place_t, combine(routes[0, 0], route_probs[0, 0]), combine(routes[0, 1], route_probs[0, 1]))
    weights, swaps, ready = gather_weights(own_weights, saved_t, ready)
    gain_col, place, weight_f, weight_b = ready
    acts = lax.all_gather(
        after(jnp.concatenate([acts_t, dy_t, saved_t], axis=0), own_weights), ("y", "c"), axis=0
    ).reshape(N_T, 3, F, TOK)
    tokens = lax.all_gather(jnp.concatenate(swaps, axis=0), ("y", "c"), axis=0).reshape(N_T, 2, F, TOK)

    bf, f32 = jnp.bfloat16, jnp.float32
    last = N_DP - N_EARLY
    block = jax.ShapeDtypeStruct((last, DS, TOK), bf)
    early_b, early_f, normal_b, normal_f, dy_last, scales = pl.pallas_call(
        early_kernel,
        in_specs=[SM] + [VM] * N_EARLY + [HB, VM],
        out_specs=[VM] * 6,
        out_shape=[
            jax.ShapeDtypeStruct((3 * G, TOK), f32),
            jax.ShapeDtypeStruct((2 * G, TOK), f32),
            block,
            block,
            block,
            jax.ShapeDtypeStruct((2, TOK), f32),
        ],
        scratch_shapes=[
            pltpu.VMEM((N_T, F, TOK), bf),
            pltpu.VMEM((N_T, F, TOK), bf),
            pltpu.VMEM((N_T, F, TOK), bf),
            pltpu.VMEM((D, TOK), bf),
            pltpu.VMEM((D, TOK), bf),
            pltpu.SemaphoreType.DMA((3,)),
        ],
        compiler_params=params(20),
        cost_estimate=cost(10 * D * G * TOK, 28 << 20),
        name="early",
    )(place, *weights[:N_EARLY], acts, gain_col)
    dg, dgs, stat = pl.pallas_call(
        inner_kernel,
        in_specs=[VM] * 7,
        out_specs=[VM] * 3,
        out_shape=[
            jax.ShapeDtypeStruct((2 * G, TOK), bf),
            jax.ShapeDtypeStruct((2 * G, TOK), bf),
            jax.ShapeDtypeStruct((1, TOK), f32),
        ],
        compiler_params=params(12),
        cost_estimate=cost(2 * D * G * TOK, 8 << 20),
        name="inner",
    )(*weights[N_EARLY:], early_b, normal_b, dy_last, weight_b, scales)
    dgs_all, tokens = gather_ring(dgs, tokens)
    payload = pl.pallas_call(
        outer_kernel,
        in_specs=[SM] + [VM] * (N_DP + 6),
        out_specs=HB,
        out_shape=jax.ShapeDtypeStruct((N_T // 2, 2, 2 * F + 2 * N_T, TOK), bf),
        scratch_shapes=[
            pltpu.VMEM((N_DP, 2, 2 * F + 2 * N_T, TOK), bf),
            pltpu.VMEM((G, TOK), bf),
            pltpu.VMEM((TOK, 2 * G), bf),
            pltpu.VMEM((TOK, G), bf),
            pltpu.SemaphoreType.DMA((N_DP,)),
        ],
        compiler_params=params(16),
        cost_estimate=cost(8 * D * G * TOK, 20 << 20),
        name="outer",
    )(place, *weights, dg, early_f, normal_f, weight_f, scales, stat)
    payload = after(payload, tuple(dgs_all[1:4]))
    summed = lax.psum_scatter(payload, "y", scatter_dimension=0)

    near_grad, far_grad = pl.pallas_call(
        grad_kernel,
        in_specs=[SM] + [VM] * (N_DP + 2),
        out_specs=[VM, VM],
        out_shape=[jax.ShapeDtypeStruct((2 * G, DS), bf)] * 2,
        compiler_params=params(12),
        cost_estimate=cost(8 * DS * G * TOK * N_DP, 8 << 20),
        name="grad",
    )(place, *dgs_all, tokens, gain[None, :])
    z = shift(near_grad, zl=1)
    behind = shift(near_grad, x=1)
    ahead = shift(near_grad, x=-1)
    z_far = shift(far_grad, zl=1)
    got = shift(summed, c=1)
    z_behind = shift(z, x=1)
    z_ahead = shift(z, x=-1)
    parts = [near_grad, z, behind, ahead, z_behind, z_ahead, far_grad, z_far]
    grad_g, grad_u = pl.pallas_call(
        assemble_kernel,
        in_specs=[SM] + [VM] * N_DP,
        out_specs=[HB, HB],
        out_shape=[jax.ShapeDtypeStruct((G, D), bf)] * 2,
        scratch_shapes=[pltpu.SemaphoreType.DMA((2 * N_DP,))],
        compiler_params=params(12),
        cost_estimate=cost(0, 8 << 20),
        name="assemble",
    )(place, *parts)

    gain_here = lax.dynamic_slice_in_dim(gain, here * F, F)[:, None]
    output, stored = pl.pallas_call(
        finish_kernel,
        in_specs=[VM] * 7,
        out_specs=[VM, VM],
        out_shape=[jax.ShapeDtypeStruct((F, TOK), bf)] * 2,
        compiler_params=params(8),
        cost_estimate=cost(20 * F * TOK, 2 << 20),
        name="finish",
    )(summed, got, acts_t, saved_t, dy_t, scales, gain_here)
    return (output.T[None], stored.T[None], grad_g.T[None], grad_u.T[None])


def solution(mesh):
    fine = Mesh(mesh.devices.reshape(tuple(SIZES[a] for a in AXES)), AXES)
    dp, tensor = ("x", "zl"), ("y", "c")
    placed = (
        P("s", dp, tensor),
        P("s", dp, tensor),
        P("s", dp, tensor),
        P("s", None),
        P("s", dp, tensor),
        P("s", dp, tensor),
        P("s", tensor, dp),
        P("s", None, dp, None),
        P("s", None, dp, None),
    )
    return jax.shard_map(
        local,
        mesh=fine,
        in_specs=placed,
        out_specs=(
            P("s", dp, tensor),
            P("s", dp, tensor),
            P("s", None, tensor),
            P("s", None, tensor),
        ),
        check_vma=False,
    )
```
